256 devices in a mesh: gx: 8 (over z_lo, core), gy: 32 (over z_hi, y, x).
Axes of the slice: x: 4, y: 4, z: 8 (z_hi: 2, z_lo: 4; z = z_hi * 4 + z_lo), core: 2. Of those that a mesh axis runs over, the one named last changes fastest.
Arguments:
- conductivity: float32 [32, 512, 16], P('gx', 'gy'), may hold values from 0.1 to 10
- storage: float32 [32, 512, 16], P('gx', 'gy'), may hold values from 0.05 to 0.5
- head_term: float32 [32, 512, 16], P('gx', 'gy'), may hold values from -6 to 6
- zone_id: int32 [32, 512, 16], P('gx', 'gy'), may hold values from 0 to 63
- layer_count: int32 [8, 32], P('gx', 'gy'), may hold values from 4 to 16, as said below
- well_cell: int32 [8, 32, 32, 8], P('gx', 'gy'), may hold values from 0 to 1023
- well_count: int32 [8, 32, 32], P('gx', 'gy'), may hold values from 0 to 8, as said below
Outputs:
- tangent: float32 [32, 512, 1024], P('gx', 'gy')
- wells: float32 [65536, 64], P(('gx', 'gy'))
The draws below stay inside these ranges and needn't reach their ends.
Inputs may be any that keep to these rules, and one draw needn't show every extreme that they name: `layer_count`: some subdomain has all 16 layers. `well_count`: in each subdomain row one owner receives 8 rows from every subdomain of that row.
All inputs are finite; a program needn't handle non-finite values.
Results may differ from the reference program's by a relative error of at most 0.0003.
Values sent between devices are 32-bit elements; how exact they have to be, the bound alone decides.
No kernel may reach another device: no remote copies, remote signals or barrier semaphores. Data moves between devices by JAX's collectives and lax.ppermute only.
A program may use at most 64 MiB of HBM per device.

```python
import math
import jax
import jax.numpy as jnp
from jax import lax

CX = 4
CY = 16
LAYERS = 16
ZONES = 64
ITERS = 3
PASSES = 4
CAP = 8
NX = 32
NY = 512
SUBX = 8
SUBY = 32
WROWS = 65536
N_GX = 8
N_GY = 32


def draw_layer_count(key, part):
    key = jax.random.fold_in(key, 5)
    first, second = jax.random.split(key)
    base = jax.random.randint(first, (N_GX, N_GY), LAYERS // 4, LAYERS + 1)
    spot = jax.random.randint(second, (), 0, N_GX * N_GY)
    places = jnp.arange(N_GX * N_GY).reshape(N_GX, N_GY)
    return jnp.where(places == spot, LAYERS, base).astype(jnp.int32)


def draw_well_count(key, part):
    key = jax.random.fold_in(key, 7)
    first, second = jax.random.split(key)
    base = jax.random.randint(first, (N_GX, N_GY, N_GY), 0, CAP + 1)
    owner = jax.random.randint(second, (N_GX,), 0, N_GY)
    dest = jnp.arange(N_GY)
    return jnp.where(dest[None, None, :] == owner[:, None, None], CAP, base).astype(jnp.int32)


def set_ends(array, own_key, least, largest):
    shape = array.shape
    place = [jax.random.randint(jax.random.fold_in(own_key, axis), (), 0, shape[axis]) for axis in range(len(shape))]
    array = array.at[tuple(place)].set(least)
    longest = shape.index(max(shape))
    place[longest] = (place[longest] + 1) % shape[longest]
    return array.at[tuple(place)].set(largest)


def block_levels(own_key, dims, cuts, smallest, top_value):
    def one(position, blocks):
        steps = jax.random.uniform(jax.random.fold_in(jax.random.fold_in(own_key, 6), position), (blocks,), jnp.float32, smallest / len(cuts), top_value / len(cuts))
        return jnp.repeat(jnp.exp(steps), dims[position] // blocks).reshape((-1,) + (1,) * (len(dims) - position - 1))

    loudness = one(*cuts[0])
    for cut in cuts[1:]:
        loudness = loudness * one(*cut)
    return loudness


def normal_values(own_key, dims, deviation, reach, cuts=(), kind=jnp.bfloat16):
    array = jax.random.normal(own_key, dims, jnp.float32) * deviation
    if len(cuts) > 0:
        array = block_levels(own_key, dims, cuts, -0.22, 0.18) * array
    return jnp.clip(array, min=-reach, max=reach).astype(kind)


def setup_inputs(seed: int = 0) -> dict:
    keys = jax.random.split(jax.random.key(seed), 8)
    return {
        "conductivity": jnp.clip(jnp.exp(math.log(10.0) - 4.6051702 * jax.random.uniform(keys[0], (NX, NY, LAYERS), jnp.float32) ** block_levels(keys[0], (NX, NY, LAYERS), ((0, 8), (1, 32)), -0.2, 0.2)), 0.1, 10.0),
        "storage": jnp.clip(jnp.exp(math.log(0.5) - 2.3025851 * jax.random.uniform(keys[1], (NX, NY, LAYERS), jnp.float32) ** block_levels(keys[1], (NX, NY, LAYERS), ((0, 8), (1, 32)), -0.2, 0.2)), 0.05, 0.5),
        "head_term": normal_values(keys[2], (NX, NY, LAYERS), 1.0, 6.0, ((0, 8), (1, 32)), jnp.float32),
        "zone_id": set_ends(jax.random.randint(keys[3], (NX, NY, LAYERS), 0, ZONES), jax.random.fold_in(keys[3], 1), 0, ZONES - 1).astype(jnp.int32),
        "layer_count": draw_layer_count(jax.random.fold_in(keys[7], 71), 0),
        "well_cell": set_ends(jax.random.randint(keys[5], (SUBX, SUBY, SUBY, CAP), 0, CX * CY * LAYERS), jax.random.fold_in(keys[5], 1), 0, (CX * CY * LAYERS) - 1).astype(jnp.int32),
        "well_count": draw_well_count(jax.random.fold_in(keys[7], 71), 0),
    }


relax_factor = 0.8

def vertical(field, stride):
    zeros = jnp.zeros_like(field[..., :stride])
    return jnp.concatenate([field[..., stride:], zeros], axis=-1) + jnp.concatenate([zeros, field[..., :-stride]], axis=-1)

def faces_sum(grid):
    return grid[:-2, 1:-1] + grid[2:, 1:-1] + grid[1:-1, :-2] + grid[1:-1, 2:]

def corner_sum(grid):
    return grid[:-2, :-2] + grid[:-2, 2:] + grid[2:, :-2] + grid[2:, 2:]

def neighbours(padded, stride):
    paired = vertical(padded, stride)
    return paired[1:-1, 1:-1] + faces_sum(padded) + 0.5 * faces_sum(paired) + 0.5 * corner_sum(padded) + 0.25 * corner_sum(paired)

def cycle_pad(field, width):
    return jnp.pad(field, ((width, width), (width, width), (0, 0)))

def spread(field, count):
    return jnp.repeat(field, count, axis=-1)

def dim_weights(length, has_lower, has_upper):
    places = jnp.arange(length)
    edge = jnp.where((places == 0) | (places == length - 1), 0.5, 1.0)
    edge = jnp.where(places == 1, jnp.where(has_lower, 0.5, 1.0), edge)
    edge = jnp.where(places == length - 2, jnp.where(has_upper, 0.5, 1.0), edge)
    return edge.astype(jnp.float32)

def prepare(cond_wide, store_ext):
    cond_ext = cond_wide[1:-1, 1:-1]
    diag_ext = store_ext + cond_ext * neighbours(cond_wide, 1)
    active = (cond_ext > 0.0).astype(jnp.float32)
    inverse = active / (diag_ext + 1.0 - active)
    return (spread(cond_ext, ZONES), spread(diag_ext, ZONES), spread(inverse, ZONES))

def sweeps(residual_ext, prepared):
    cond_full, diag_full, inverse_full = prepared
    correction = jnp.zeros_like(residual_ext)
    for sweep in range(PASSES):
        applied = diag_full * correction - cond_full * neighbours(cycle_pad(cond_full * correction, 1), ZONES)
        correction = correction + relax_factor * inverse_full * (residual_ext - applied)
    return correction

def reference(conductivity, storage, head_term, zone_id, layer_count, well_cell, well_count):
    depth = jnp.arange(LAYERS, dtype=jnp.int32)
    layers_cell = jnp.repeat(jnp.repeat(layer_count, CX, axis=0), CY, axis=1)
    active = (depth[None, None, :] < layers_cell[:, :, None]).astype(jnp.float32)
    cond = jnp.sqrt(conductivity) * active
    onehot = (zone_id[..., None] == jnp.arange(ZONES, dtype=jnp.int32)).astype(jnp.float32)
    source = (onehot * (cond * head_term)[..., None]).reshape(NX, NY, LAYERS * ZONES)
    diag = storage + cond * neighbours(cycle_pad(cond, 1), 1)
    cond_full = spread(cond, ZONES)
    diag_full = spread(diag, ZONES)
    cond_wide = cycle_pad(cond, 2)
    store_wide = cycle_pad(storage, 2)
    tangent = jnp.zeros((NX, NY, LAYERS * ZONES), jnp.float32)
    anchor = jnp.zeros((), jnp.int32)
    for outer in range(ITERS):
        residual = source - (diag_full * tangent - cond_full * neighbours(cycle_pad(cond_full * tangent, 1), ZONES))
        resid_pad = cycle_pad(residual, 1)

        def add_one(index, total):
            row = (index // N_GY).astype(jnp.int32)
            col = (index % N_GY).astype(jnp.int32)
            start_row = (row * CX).astype(jnp.int32)
            start_col = (col * CY).astype(jnp.int32)
            sub_res = lax.dynamic_slice(resid_pad, (start_row, start_col, anchor), (CX + 2, CY + 2, LAYERS * ZONES))
            sub_cond = lax.dynamic_slice(cond_wide, (start_row, start_col, anchor), (CX + 4, CY + 4, LAYERS))
            sub_store = lax.dynamic_slice(store_wide, (start_row, start_col, anchor), (CX + 4, CY + 4, LAYERS))[1:-1, 1:-1]
            correction = sweeps(sub_res, prepare(sub_cond, sub_store))
            weights = dim_weights(CX + 2, row > 0, row < N_GX - 1)[:, None, None] * dim_weights(CY + 2, col > 0, col < N_GY - 1)[None, :, None]
            current = lax.dynamic_slice(total, (start_row, start_col, anchor), (CX + 2, CY + 2, LAYERS * ZONES))
            return lax.dynamic_update_slice(total, current + weights * correction, (start_row, start_col, anchor))
        total = lax.fori_loop(0, N_GX * N_GY, add_one, jnp.zeros((NX + 2, NY + 2, LAYERS * ZONES), jnp.float32))
        tangent = tangent + total[1:-1, 1:-1]
    blocks = tangent.reshape(N_GX, CX, N_GY, CY, LAYERS, ZONES).transpose(0, 2, 1, 3, 4, 5).reshape(N_GX * N_GY, CX * CY * LAYERS, ZONES)
    cells = well_cell.reshape(N_GX * N_GY, N_GY * CAP).astype(jnp.int32)
    picks = jax.vmap(lambda table, places: jnp.take(table, places, axis=0))(blocks, cells)
    picks = picks.reshape(N_GX, N_GY, N_GY, CAP, ZONES)
    live = (jnp.arange(CAP, dtype=jnp.int32)[None, None, None, :] < well_count[..., None]).astype(jnp.float32)
    picks = picks * live[..., None]
    wells = picks.transpose(0, 2, 1, 3, 4).reshape(WROWS, ZONES)
    return (tangent, wells)
```

```python
import jax
import jax.numpy as jnp
from jax import lax
from jax.experimental import pallas as pl
from jax.experimental.pallas import tpu as pltpu
from jax.sharding import PartitionSpec as P

ROWS, COLS, LAYERS, ZONES = 4, 16, 16, 64
HALO = 12
WIDE = COLS + 2 * HALO
PAIRS = WIDE // 2
SUBX, SUBY = 8, 32
GROUP = ZONES // SUBX
TILE = (SUBX, LAYERS * GROUP)
STEP = 3
RELAX = 0.8


def total(first, second):
    return first if second is None else second if first is None else first + second


def lane_places():
    return lax.broadcasted_iota(jnp.int32, TILE, 1)


def sub_places():
    return lax.broadcasted_iota(jnp.int32, TILE, 0)


def up_sub(field):
    return jnp.where(sub_places() == 0, 0.0, pltpu.roll(field, 1, 0))


def down_sub(field):
    return jnp.where(sub_places() == SUBX - 1, 0.0, pltpu.roll(field, SUBX - 1, 0))


def layers_sum(field):
    lanes = lane_places()
    above = jnp.where(lanes >= TILE[1] - GROUP, 0.0, pltpu.roll(field, TILE[1] - GROUP, 1))
    below = jnp.where(lanes < GROUP, 0.0, pltpu.roll(field, GROUP, 1))
    return (field + above) + (field + below)


def rows_sum(cells):
    pairs = [total(a, b) for a, b in zip(cells[:-1], cells[1:])]
    return [total(a, b) for a, b in zip(pairs[:-1], pairs[1:])]


def column_loop(first, last, column, emit):
    before = column(first - 1)
    here = column(first)
    pair = [a + b for a, b in zip(before, here)]

    def one(col, here, pair):
        after = column(col + 1)
        next_pair = [a + b for a, b in zip(here, after)]
        emit(col, [a + b for a, b in zip(pair, next_pair)])
        return after, next_pair

    count = last + 1 - first
    groups = count // STEP

    def body(index, carry):
        here, pair = carry
        for inner in range(STEP):
            here, pair = one(first + index * STEP + inner, here, pair)
        return here, pair

    if groups > 1:
        here, pair = lax.fori_loop(0, groups, body, (here, pair))
        first = first + groups * STEP
    for col in range(first, last + 1):
        here, pair = one(col, here, pair)


def expand(raw, cond, store, head, zone):
    lanes = lane_places()
    picks = [[side * 64 + part * LAYERS + lanes // GROUP for part in range(4)] for side in range(2)]

    def body(index, carry):
        for side in range(2):
            col = 2 * index + side
            conds = []
            for row in range(ROWS):
                packed = raw[pl.ds(row * PAIRS + index, SUBX, stride=ROWS * PAIRS), :]
                parts = [
                    jnp.take_along_axis(packed, places, axis=1, mode="promise_in_bounds")
                    for places in picks[side]
                ]
                conds.append(parts[0])
                store[col, row] = parts[1]
                head[col, row] = parts[2]
                zone[col, row] = parts[3]
            for row, field in enumerate([up_sub(conds[-1])] + conds + [down_sub(conds[0])]):
                cond[col, row] = field
        return carry

    lax.fori_loop(0, PAIRS, body, 0)


def coefficients(zone_base, cond, store, head, zone, keep, gain, source):
    wanted = (zone_base + lane_places() % GROUP).astype(jnp.float32)

    def column(col):
        sums = rows_sum([cond[col, row] for row in range(ROWS + 2)])
        return [layers_sum(field) for field in sums]

    def emit(col, around):
        keeps, gains, sources = [], [], []
        for row in range(ROWS):
            here = cond[col, row + 1]
            near = here * (0.25 * around[row])
            diag = store[col, row] + (near - 2.0 * here * here)
            active = jnp.where(here > 0.0, 1.0, 0.0)
            step = RELAX * (active / (diag + 1.0 - active))
            scaled = step * here * here
            keeps.append(1.0 - step * (store[col, row] + near))
            gains.append(0.25 * scaled)
            sources.append(jnp.where(zone[col, row] == wanted, scaled * head[col, row], 0.0))
        for target, fields in ((keep, keeps), (gain, gains), (source, sources)):
            for row, field in enumerate([up_sub(fields[-1])] + fields + [down_sub(fields[0])]):
                target[col, row] = field

    column_loop(1, WIDE - 2, column, emit)


def main_kernel(info, raw, out, cond, store, head, zone, keep, gain, source, state, *buffers):
    expand(raw, cond, store, head, zone)
    coefficients(info[0], cond, store, head, zone, keep, gain, source)
    has_left, has_right = info[1] > 0, info[2] > 0
    left_own = jnp.where(has_left, 0.5, 1.0)
    right_own = jnp.where(has_right, 0.5, 1.0)
    subs = sub_places()
    low_own = jnp.where(subs == 0, 1.0, 0.5)
    high_own = jnp.where(subs == SUBX - 1, 1.0, 0.5)
    high = HALO + COLS
    bases = (0, HALO - 2, high - 2)
    ends = (HALO + 1, high + 1, WIDE - 1)
    rims = ((HALO + 1,), (HALO - 2, high + 1), (high - 2,))
    fields = tuple((buffers[2 * k], buffers[2 * k + 1]) for k in range(3))
    zeros = jnp.zeros(TILE, jnp.float32)

    for outer in range(3):
        reach = 4 * (2 - outer)
        for part in range(3):
            for buffer in fields[part]:
                for col in rims[part]:
                    for row in range(6):
                        buffer[col - bases[part], row] = zeros if outer == 0 else state[col, row + 1]
        for sweep in range(4):
            more = reach + 3 - sweep
            ranges = (
                (HALO - more, HALO),
                (HALO - 1, high) if more > 0 else (HALO, high - 1),
                (high - 1, high - 1 + more),
            )
            for part in range(3):
                base = bases[part]
                old, new = fields[part][(sweep + 1) % 2], fields[part][sweep % 2]
                first, last = ranges[part]
                if outer == 0 and sweep == 0:
                    def copy(col, carry, new=new, base=base):
                        for row in range(6):
                            new[col - base, row] = source[col, row]
                        return carry
                    lax.fori_loop(first, last + 1, copy, 0)
                    continue

                def column(col, old=old, base=base, sweep=sweep, outer=outer):
                    if sweep == 0:
                        cells = [state[col, row] for row in range(8)]
                    else:
                        cells = [old[col - base, row] for row in range(6)]
                        if outer == 0:
                            cells = [None] + cells + [None]
                        else:
                            cells = [state[col, 0]] + cells + [state[col, 7]]
                    return [layers_sum(field) for field in rows_sum(cells)]

                def emit(col, around, old=old, new=new, base=base, sweep=sweep):
                    for row in range(6):
                        here = state[col, row + 1] if sweep == 0 else old[col - base, row]
                        new[col - base, row] = (
                            source[col, row] + keep[col, row] * here + gain[col, row] * around[row]
                        )

                column_loop(first, last, column, emit)

        done = tuple(fields[part][1] for part in range(3))

        def merge(col, cells, final):
            mine = [
                low_own * cells[1] + (1.0 - low_own) * pltpu.roll(cells[5], 1, 0),
                cells[2],
                cells[3],
                high_own * cells[4] + (1.0 - high_own) * pltpu.roll(cells[0], SUBX - 1, 0),
            ]
            if final:
                for row in range(ROWS):
                    here = cond[col, row + 1]
                    inside = here > 0.0
                    value = jnp.where(inside, mine[row] / jnp.where(inside, here, 1.0), 0.0)
                    out[pl.ds(row * COLS + col - HALO, SUBX, stride=ROWS * COLS), :] = value
            else:
                for row in range(ROWS):
                    state[col, row + 2] = mine[row]
                state[col, 0] = up_sub(mine[2])
                state[col, 1] = up_sub(mine[3])
                state[col, 6] = down_sub(mine[0])
                state[col, 7] = down_sub(mine[1])

        def merge_range(first, last, part):
            def body(col, carry):
                merge(col, [done[part][col - bases[part], row] for row in range(6)], outer == 2)
                return carry
            lax.fori_loop(first, last + 1, body, 0)

        def merge_mixed(col, part, own):
            cells = [
                own * done[1][col - bases[1], row] + (1.0 - own) * done[part][col - bases[part], row]
                for row in range(6)
            ]
            merge(col, cells, outer == 2)

        lefts = (HALO - 1, HALO) if outer < 2 else (HALO,)
        rights = (high - 1, high) if outer < 2 else (high - 1,)
        for col in lefts:
            merge_mixed(col, 0, left_own)
        for col in rights:
            merge_mixed(col, 2, right_own)
        merge_range(HALO + 1, high - 2, 1)
        if outer < 2:
            merge_range(HALO - reach, HALO - 2, 0)
            merge_range(high + 1, high - 1 + reach, 2)


def run_main(info, raw):
    def cells(cols, rows):
        return pltpu.VMEM((cols, rows) + TILE, jnp.float32)

    scratch = [cells(WIDE, 6)] + [cells(WIDE, ROWS)] * 3 + [cells(WIDE, 6)] * 3 + [cells(WIDE, 8)]
    scratch += [cells(HALO + 2, 6)] * 2 + [cells(COLS + 4, 6)] * 2 + [cells(HALO + 2, 6)] * 2
    return pl.pallas_call(
        main_kernel,
        out_shape=jax.ShapeDtypeStruct((SUBX * ROWS * COLS, TILE[1]), jnp.float32),
        in_specs=[pl.BlockSpec(memory_space=pltpu.SMEM), pl.BlockSpec(memory_space=pltpu.VMEM)],
        out_specs=pl.BlockSpec(memory_space=pltpu.VMEM),
        scratch_shapes=scratch,
        compiler_params=pltpu.CompilerParams(vmem_limit_bytes=40 * 1024 * 1024),
        name="schwarz",
    )(info, raw)


def place_kernel(parts, tangent):
    lanes = lane_places()
    rows = ROWS * COLS

    def body(index, carry):
        start = pl.multiple_of(index * 8, 8)
        blocks = [parts[pl.ds(pl.multiple_of(a * rows + index * 8, 8), 8), :] for a in range(SUBX)]
        for pair in range(LAYERS // 2):
            places = (2 * pair + lanes // ZONES) * GROUP + lanes % GROUP
            whole = jnp.zeros(TILE, jnp.float32)
            for a in range(SUBX):
                moved = jnp.take_along_axis(blocks[a], places, axis=1, mode="promise_in_bounds")
                whole = jnp.where((lanes % ZONES) // GROUP == a, moved, whole)
            tangent[pl.ds(start, 8), pair * 128 : (pair + 1) * 128] = whole
        return carry

    lax.fori_loop(0, rows // 8, body, 0)


def run_place(parts):
    return pl.pallas_call(
        place_kernel,
        out_shape=jax.ShapeDtypeStruct((ROWS * COLS, LAYERS * ZONES), jnp.float32),
        in_specs=[pl.BlockSpec(memory_space=pltpu.VMEM)],
        out_specs=pl.BlockSpec(memory_space=pltpu.VMEM),
        name="place",
    )(parts)


def gather_inputs(conductivity, storage, head_term, zone_id, layer_count):
    depth = jnp.arange(LAYERS, dtype=jnp.int32)
    active = (depth[None, None, :] < layer_count[0, 0]).astype(jnp.float32)
    cond = jnp.sqrt(conductivity) * active
    fields = jnp.concatenate([cond, storage, head_term, zone_id.astype(jnp.float32)], axis=2)
    even = lax.axis_index("gy") % 2 == 0
    inner = [(i, i ^ 1) for i in range(SUBY)]
    outer = [(i, i + 1) for i in range(1, SUBY - 1, 2)]
    outer = outer + [(j, i) for i, j in outer]
    first, last = fields[:, :HALO], fields[:, COLS - HALO :]
    got_inner = lax.ppermute(jnp.where(even, last, first), "gy", inner)
    got_outer = lax.ppermute(jnp.where(even, first, last), "gy", outer)
    left = jnp.where(even, got_outer, got_inner)
    right = jnp.where(even, got_inner, got_outer)
    wide = jnp.concatenate([left, fields, right], axis=1).reshape(ROWS * PAIRS, 128)
    copies = jnp.broadcast_to(wide[None], (SUBX,) + wide.shape)
    gathered = lax.all_to_all(copies, "gx", 0, 0, tiled=True)
    return gathered.reshape(SUBX * ROWS * PAIRS, 128)


def shards(conductivity, storage, head_term, zone_id, layer_count, well_cell, well_count):
    raw = gather_inputs(conductivity, storage, head_term, zone_id, layer_count)
    row, col = lax.axis_index("gx"), lax.axis_index("gy")
    info = jnp.stack([row * GROUP, col, SUBY - 1 - col]).astype(jnp.int32)
    parts = run_main(info, raw).reshape(SUBX, ROWS * COLS, 128)
    parts = lax.all_to_all(parts, "gx", 0, 0, tiled=True)
    tangent = run_place(parts.reshape(SUBX * ROWS * COLS, 128)).reshape(ROWS, COLS, LAYERS * ZONES)
    flat = tangent.reshape(ROWS * COLS * LAYERS, ZONES)
    owners, slots = well_cell.shape[2:]
    cells = well_cell[0, 0].reshape(owners * slots)
    picked = jnp.take(flat, cells, axis=0).reshape(owners, slots, ZONES)
    live = jnp.arange(slots, dtype=jnp.int32)[None, :] < well_count[0, 0][:, None]
    picked = jnp.where(live[..., None], picked, 0.0)
    arrived = lax.all_to_all(picked, "gy", split_axis=0, concat_axis=0, tiled=True)
    return (tangent, arrived.reshape(owners * slots, ZONES))


def solution(mesh):
    placed = (
        P("gx", "gy", None),
        P("gx", "gy", None),
        P("gx", "gy", None),
        P("gx", "gy", None),
        P("gx", "gy"),
        P("gx", "gy", None, None),
        P("gx", "gy", None),
    )
    return jax.shard_map(
        shards,
        mesh=mesh,
        in_specs=placed,
        out_specs=(P("gx", "gy", None), P(("gx", "gy"), None)),
        check_vma=False,
    )
```

```python
import jax
import jax.numpy as jnp
from jax import lax
from jax.experimental import pallas as pl
from jax.experimental.pallas import tpu as pltpu
from jax.sharding import PartitionSpec as P

ROWS, COLS, LAYERS, ZONES = 4, 16, 16, 64
HALO = 12
WIDE = COLS + 2 * HALO
PAIRS = WIDE // 2
SUBX, SUBY = 8, 32
CAP = 8
GROUP = ZONES // SUBX
TILE = (SUBX, LAYERS * GROUP)
RELAX = 0.8


def total(first, second):
    return first if second is None else second if first is None else first + second


def lane_places():
    return lax.broadcasted_iota(jnp.int32, TILE, 1)


def sub_places():
    return lax.broadcasted_iota(jnp.int32, TILE, 0)


def up_sub(field):
    return jnp.where(sub_places() == 0, 0.0, pltpu.roll(field, 1, 0))


def down_sub(field):
    return jnp.where(sub_places() == SUBX - 1, 0.0, pltpu.roll(field, SUBX - 1, 0))


def layers_sum(field):
    lanes = lane_places()
    above = jnp.where(lanes >= TILE[1] - GROUP, 0.0, pltpu.roll(field, TILE[1] - GROUP, 1))
    below = jnp.where(lanes < GROUP, 0.0, pltpu.roll(field, GROUP, 1))
    return (field + above) + (field + below)


def rows_sum(cells):
    pairs = [total(a, b) for a, b in zip(cells[:-1], cells[1:])]
    return [total(a, b) for a, b in zip(pairs[:-1], pairs[1:])]


def column_loop(first, last, column, emit):
    before = column(first - 1)
    here = column(first)
    pair = [a + b for a, b in zip(before, here)]

    def one(col, here, pair):
        after = column(col + 1)
        next_pair = [a + b for a, b in zip(here, after)]
        emit(col, [a + b for a, b in zip(pair, next_pair)])
        return after, next_pair

    for col in range(first, last + 1):
        here, pair = one(col, here, pair)


def expand(raw, cond, store, head, zone):
    lanes = lane_places()
    picks = [[side * 64 + part * LAYERS + lanes // GROUP for part in range(4)] for side in range(2)]

    def body(index, carry):
        for side in range(2):
            col = 2 * index + side
            conds = []
            for row in range(ROWS):
                packed = raw[pl.ds(row * PAIRS + index, SUBX, stride=ROWS * PAIRS), :]
                parts = [
                    jnp.take_along_axis(packed, places, axis=1, mode="promise_in_bounds")
                    for places in picks[side]
                ]
                conds.append(parts[0])
                store[col, row] = parts[1]
                head[col, row] = parts[2]
                zone[col, row] = parts[3]
            for row, field in enumerate([up_sub(conds[-1])] + conds + [down_sub(conds[0])]):
                cond[col, row] = field
        return carry

    lax.fori_loop(0, PAIRS, body, 0, unroll=True)


def coefficients(zone_base, cond, store, head, zone, keep, gain, source):
    wanted = (zone_base + lane_places() % GROUP).astype(jnp.float32)

    def column(col):
        sums = rows_sum([cond[col, row] for row in range(ROWS + 2)])
        return [layers_sum(field) for field in sums]

    def emit(col, around):
        keeps, gains, sources = [], [], []
        for row in range(ROWS):
            here = cond[col, row + 1]
            near = here * (0.25 * around[row])
            diag = store[col, row] + (near - 2.0 * here * here)
            active = jnp.where(here > 0.0, 1.0, 0.0)
            step = RELAX * (active / (diag + 1.0 - active))
            scaled = step * here * here
            keeps.append(1.0 - step * (store[col, row] + near))
            gains.append(0.25 * scaled)
            sources.append(jnp.where(zone[col, row] == wanted, scaled * head[col, row], 0.0))
        for target, fields in ((keep, keeps), (gain, gains), (source, sources)):
            for row, field in enumerate([up_sub(fields[-1])] + fields + [down_sub(fields[0])]):
                target[col, row] = field

    column_loop(1, WIDE - 2, column, emit)


def collect(me, mine, other, raw):
    block = ROWS * PAIRS
    for place in range(SUBX):
        piece = (mine if place % 2 == 0 else other)[pl.ds((place // 2) * block, block), :]
        raw[pl.ds(pl.multiple_of((me ^ place) * block, 8), block), :] = piece


def main_kernel(info, mine, other, out, raw, cond, store, head, zone, keep, gain, source, state, *buffers):
    collect(info[0], mine, other, raw)
    expand(raw, cond, store, head, zone)
    coefficients(info[0] * GROUP, cond, store, head, zone, keep, gain, source)
    has_left, has_right = info[1] > 0, info[2] > 0
    left_own = jnp.where(has_left, 0.5, 1.0)
    right_own = jnp.where(has_right, 0.5, 1.0)
    subs = sub_places()
    low_own = jnp.where(subs == 0, 1.0, 0.5)
    high_own = jnp.where(subs == SUBX - 1, 1.0, 0.5)
    high = HALO + COLS
    bases = (0, HALO - 2, high - 2)
    ends = (HALO + 1, high + 1, WIDE - 1)
    rims = ((HALO + 1,), (HALO - 2, high + 1), (high - 2,))
    fields = tuple((buffers[2 * k], buffers[2 * k + 1]) for k in range(3))
    zeros = jnp.zeros(TILE, jnp.float32)

    for outer in range(3):
        reach = 4 * (2 - outer)
        for part in range(3):
            for buffer in fields[part]:
                for col in rims[part]:
                    for row in range(6):
                        buffer[col - bases[part], row] = zeros if outer == 0 else state[col, row + 1]
        for sweep in range(4):
            more = reach + 3 - sweep
            ranges = (
                (HALO - more, HALO),
                (HALO - 1, high) if more > 0 else (HALO, high - 1),
                (high - 1, high - 1 + more),
            )
            for part in range(3):
                base = bases[part]
                old, new = fields[part][(sweep + 1) % 2], fields[part][sweep % 2]
                first, last = ranges[part]
                if outer == 0 and sweep == 0:
                    def copy(col, carry, new=new, base=base):
                        for row in range(6):
                            new[col - base, row] = source[col, row]
                        return carry
                    lax.fori_loop(first, last + 1, copy, 0, unroll=True)
                    continue

                def column(col, old=old, base=base, sweep=sweep, outer=outer):
                    if sweep == 0:
                        cells = [state[col, row] for row in range(8)]
                    else:
                        cells = [old[col - base, row] for row in range(6)]
                        if outer == 0:
                            cells = [None] + cells + [None]
                        else:
                            cells = [state[col, 0]] + cells + [state[col, 7]]
                    return [layers_sum(field) for field in rows_sum(cells)]

                def emit(col, around, old=old, new=new, base=base, sweep=sweep):
                    for row in range(6):
                        here = state[col, row + 1] if sweep == 0 else old[col - base, row]
                        new[col - base, row] = (
                            source[col, row] + keep[col, row] * here + gain[col, row] * around[row]
                        )

                column_loop(first, last, column, emit)

        done = tuple(fields[part][1] for part in range(3))

        def merge(col, cells, final):
            mine = [
                low_own * cells[1] + (1.0 - low_own) * pltpu.roll(cells[5], 1, 0),
                cells[2],
                cells[3],
                high_own * cells[4] + (1.0 - high_own) * pltpu.roll(cells[0], SUBX - 1, 0),
            ]
            if final:
                for row in range(ROWS):
                    here = cond[col, row + 1]
                    inside = here > 0.0
                    value = jnp.where(inside, mine[row] / jnp.where(inside, here, 1.0), 0.0)
                    out[pl.ds(row * COLS + col - HALO, SUBX, stride=ROWS * COLS), :] = value
            else:
                for row in range(ROWS):
                    state[col, row + 2] = mine[row]
                state[col, 0] = up_sub(mine[2])
                state[col, 1] = up_sub(mine[3])
                state[col, 6] = down_sub(mine[0])
                state[col, 7] = down_sub(mine[1])

        def merge_range(first, last, part):
            def body(col, carry):
                merge(col, [done[part][col - bases[part], row] for row in range(6)], outer == 2)
                return carry
            lax.fori_loop(first, last + 1, body, 0, unroll=True)

        def merge_mixed(col, part, own):
            cells = [
                own * done[1][col - bases[1], row] + (1.0 - own) * done[part][col - bases[part], row]
                for row in range(6)
            ]
            merge(col, cells, outer == 2)

        lefts = (HALO - 1, HALO) if outer < 2 else (HALO,)
        rights = (high - 1, high) if outer < 2 else (high - 1,)
        for col in lefts:
            merge_mixed(col, 0, left_own)
        for col in rights:
            merge_mixed(col, 2, right_own)
        merge_range(HALO + 1, high - 2, 1)
        if outer < 2:
            merge_range(HALO - reach, HALO - 2, 0)
            merge_range(high + 1, high - 1 + reach, 2)


def run_main(info, mine, other):
    def cells(cols, rows):
        return pltpu.VMEM((cols, rows) + TILE, jnp.float32)

    scratch = [pltpu.VMEM((SUBX * ROWS * PAIRS, 128), jnp.float32), cells(WIDE, 6)] + [cells(WIDE, ROWS)] * 3 + [cells(WIDE, 6)] * 3 + [cells(WIDE, 8)]
    scratch += [cells(HALO + 2, 6)] * 2 + [cells(COLS + 4, 6)] * 2 + [cells(HALO + 2, 6)] * 2
    return pl.pallas_call(
        main_kernel,
        out_shape=jax.ShapeDtypeStruct((SUBX * ROWS * COLS, TILE[1]), jnp.float32),
        in_specs=[pl.BlockSpec(memory_space=pltpu.SMEM)] + [pl.BlockSpec(memory_space=pltpu.VMEM)] * 2,
        out_specs=pl.BlockSpec(memory_space=pltpu.VMEM),
        scratch_shapes=scratch,
        compiler_params=pltpu.CompilerParams(vmem_limit_bytes=40 * 1024 * 1024),
        name="schwarz",
    )(info, mine, other)


def place_kernel(cells, counts, parts, tangent, picks, table):
    lanes = lane_places()
    rows = ROWS * COLS

    def body(index, carry):
        start = pl.multiple_of(index * 8, 8)
        blocks = [parts[pl.ds(pl.multiple_of(a * rows + index * 8, 8), 8), :] for a in range(SUBX)]
        for pair in range(LAYERS // 2):
            places = (2 * pair + lanes // ZONES) * GROUP + lanes % GROUP
            whole = jnp.zeros(TILE, jnp.float32)
            for a in range(SUBX):
                moved = jnp.take_along_axis(blocks[a], places, axis=1, mode="promise_in_bounds")
                whole = jnp.where((lanes % ZONES) // GROUP == a, moved, whole)
            tangent[pl.ds(start, 8), pair * 128 : (pair + 1) * 128] = whole
            table[pl.ds(pl.multiple_of(pair * rows + index * 8, 8), 8), :] = whole
        return carry

    lax.fori_loop(0, rows // 8, body, 0, unroll=2)
    upper = lax.broadcasted_iota(jnp.int32, (1, 128), 1) >= ZONES

    def fetch(owner, slot, want):
        cell = cells[slot, owner]
        layer = cell % LAYERS
        line = table[pl.ds((layer // 2) * rows + cell // LAYERS, 1), :]
        line = jnp.where(layer % 2 == want, line, pltpu.roll(line, ZONES, 1))
        return jnp.where(slot < counts[owner], line, 0.0)

    def pick(owner, carry):
        lines = []
        for slot in range(CAP // 2):
            lines.append(jnp.where(upper, fetch(owner, slot + CAP // 2, 1), fetch(owner, slot, 0)))
        for slot, line in enumerate(lines):
            picks[pl.ds(owner * (CAP // 2) + slot, 1), :] = line
        return carry

    lax.fori_loop(0, SUBY, pick, 0, unroll=4)


def run_place(cells, counts, parts):
    return pl.pallas_call(
        place_kernel,
        out_shape=(
            jax.ShapeDtypeStruct((ROWS * COLS, LAYERS * ZONES), jnp.float32),
            jax.ShapeDtypeStruct((SUBY * CAP // 2, 128), jnp.float32),
        ),
        in_specs=[pl.BlockSpec(memory_space=pltpu.SMEM)] * 2 + [pl.BlockSpec(memory_space=pltpu.VMEM)],
        out_specs=(pl.BlockSpec(memory_space=pltpu.VMEM),) * 2,
        scratch_shapes=[pltpu.VMEM((ROWS * COLS * LAYERS // 2, 128), jnp.float32)],
        name="place",
    )(cells, counts, parts)


def finish_kernel(arrived, wells):
    across = arrived[...].T
    lanes = lane_places()
    for start in range(0, ZONES, 8):
        low, high = across[start : start + 8], across[ZONES + start : ZONES + start + 8]
        for half in range(2):
            places = (half * 16 + lanes // CAP) * (CAP // 2) + lanes % (CAP // 2)
            both = [
                jnp.take_along_axis(part, places, axis=1, mode="promise_in_bounds") for part in (low, high)
            ]
            wells[start : start + 8, half * 128 : (half + 1) * 128] = jnp.where(
                lanes % CAP < CAP // 2, both[0], both[1]
            )


def run_finish(arrived):
    return pl.pallas_call(
        finish_kernel,
        out_shape=jax.ShapeDtypeStruct((ZONES, SUBY * CAP), jnp.float32),
        in_specs=[pl.BlockSpec(memory_space=pltpu.VMEM)],
        out_specs=pl.BlockSpec(memory_space=pltpu.VMEM),
        name="finish",
    )(arrived)


def gather_inputs(conductivity, storage, head_term, zone_id, layer_count):
    depth = jnp.arange(LAYERS, dtype=jnp.int32)
    active = (depth[None, None, :] < layer_count[0, 0]).astype(jnp.float32)
    cond = jnp.sqrt(conductivity) * active
    fields = jnp.concatenate([cond, storage, head_term, zone_id.astype(jnp.float32)], axis=2)
    even = lax.axis_index("gy") % 2 == 0
    inner = [(i, i ^ 1) for i in range(SUBY)]
    outer = [(i, i + 1) for i in range(1, SUBY - 1, 2)]
    outer = outer + [(j, i) for i, j in outer]
    first, last = fields[:, :HALO], fields[:, COLS - HALO :]
    got_inner = lax.ppermute(jnp.where(even, last, first), "gy", inner)
    got_outer = lax.ppermute(jnp.where(even, first, last), "gy", outer)
    left = jnp.where(even, got_outer, got_inner)
    right = jnp.where(even, got_inner, got_outer)
    wide = jnp.concatenate([left, fields, right], axis=1).reshape(ROWS * PAIRS, 128)
    blocks = [wide]
    for shift in (2, 4, 6):
        blocks.append(lax.ppermute(wide, "gx", [(i, i ^ shift) for i in range(SUBX)]))
    mine = jnp.concatenate(blocks, axis=0)
    other = lax.ppermute(mine, "gx", [(i, i ^ 1) for i in range(SUBX)])
    return mine, other


def shards(conductivity, storage, head_term, zone_id, layer_count, well_cell, well_count):
    mine, other = gather_inputs(conductivity, storage, head_term, zone_id, layer_count)
    row, col = lax.axis_index("gx"), lax.axis_index("gy")
    info = jnp.stack([row, col, SUBY - 1 - col]).astype(jnp.int32)
    parts = run_main(info, mine, other).reshape(SUBX, ROWS * COLS, 128)
    parts = lax.all_to_all(parts, "gx", 0, 0, tiled=True)
    tangent, picks = run_place(
        well_cell[0, 0].T, well_count[0, 0], parts.reshape(SUBX * ROWS * COLS, 128)
    )
    picks = picks.reshape(SUBY, CAP // 2, 128)
    arrived = lax.all_to_all(picks, "gy", split_axis=0, concat_axis=0, tiled=True)
    wells = run_finish(arrived.reshape(SUBY * CAP // 2, 128)).T
    return (tangent.reshape(ROWS, COLS, LAYERS * ZONES), wells)


def solution(mesh):
    placed = (
        P("gx", "gy", None),
        P("gx", "gy", None),
        P("gx", "gy", None),
        P("gx", "gy", None),
        P("gx", "gy"),
        P("gx", "gy", None, None),
        P("gx", "gy", None),
    )
    return jax.shard_map(
        shards,
        mesh=mesh,
        in_specs=placed,
        out_specs=(P("gx", "gy", None), P(("gx", "gy"), None)),
        check_vma=False,
    )
```

```python
import jax
import jax.numpy as jnp
from jax import lax
from jax.experimental import pallas as pl
from jax.experimental.pallas import tpu as pltpu
from jax.sharding import PartitionSpec as P

ROWS, COLS, LAYERS, ZONES = 4, 16, 16, 64
HALO = 12
WIDE = COLS + 2 * HALO
HALF = COLS // 2
OWN = ROWS * HALF
BLOCK = 3 * OWN
PLACES = ROWS * COLS
SUBX, SUBY = 8, 32
CAP = 8
GROUP = ZONES // SUBX
TILE = (SUBX, LAYERS * GROUP)
RELAX = 0.8


def total(first, second):
    return first if second is None else second if first is None else first + second


def lane_places():
    return lax.broadcasted_iota(jnp.int32, TILE, 1)


def sub_places():
    return lax.broadcasted_iota(jnp.int32, TILE, 0)


def up_sub(field):
    return jnp.where(sub_places() == 0, 0.0, pltpu.roll(field, 1, 0))


def down_sub(field):
    return jnp.where(sub_places() == SUBX - 1, 0.0, pltpu.roll(field, SUBX - 1, 0))


def layers_sum(field):
    lanes = lane_places()
    above = jnp.where(lanes >= TILE[1] - GROUP, 0.0, pltpu.roll(field, TILE[1] - GROUP, 1))
    below = jnp.where(lanes < GROUP, 0.0, pltpu.roll(field, GROUP, 1))
    return (field + above) + (field + below)


def rows_sum(cells):
    pairs = [total(a, b) for a, b in zip(cells[:-1], cells[1:])]
    return [total(a, b) for a, b in zip(pairs[:-1], pairs[1:])]


def column_loop(first, last, column, emit):
    before = column(first - 1)
    here = column(first)
    pair = [a + b for a, b in zip(before, here)]

    def one(col, here, pair):
        after = column(col + 1)
        next_pair = [a + b for a, b in zip(here, after)]
        emit(col, [a + b for a, b in zip(pair, next_pair)])
        return after, next_pair

    for col in range(first, last + 1):
        here, pair = one(col, here, pair)


def pack_kernel(layers, conductivity, storage, head, zone, own):
    live = lax.broadcasted_iota(jnp.int32, (HALF, LAYERS), 1) < layers[0, 0]
    for row in range(ROWS):
        parts = []
        for half in range(2):
            cols = slice(half * HALF, (half + 1) * HALF)
            parts.append(jnp.where(live, jnp.sqrt(conductivity[row, cols, :]), 0.0))
            parts.append(storage[row, cols, :])
            parts.append(head[row, cols, :])
            parts.append(zone[row, cols, :].astype(jnp.float32))
        own[row * HALF : (row + 1) * HALF, :] = jnp.concatenate(parts, axis=1)


def run_pack(layers, conductivity, storage, head, zone):
    return pl.pallas_call(
        pack_kernel,
        out_shape=jax.ShapeDtypeStruct((OWN, 128), jnp.float32),
        in_specs=[pl.BlockSpec(memory_space=pltpu.SMEM)] + [pl.BlockSpec(memory_space=pltpu.VMEM)] * 4,
        out_specs=pl.BlockSpec(memory_space=pltpu.VMEM),
        name="pack",
    )(layers, conductivity, storage, head, zone)


def expand(odd, raw, cond, store, head, zone):
    lanes = lane_places()
    picks = [[half * 64 + part * LAYERS + lanes // GROUP for part in range(4)] for half in range(2)]
    bases = (2 * OWN - odd * OWN, 0, OWN + odd * OWN)

    for col in range(WIDE):
        block, place = divmod(col - HALO + COLS, COLS)
        conds = []
        for row in range(ROWS):
            packed = raw[pl.ds(bases[block] + row * HALF + place % HALF, SUBX, stride=BLOCK), :]
            parts = [
                jnp.take_along_axis(packed, places, axis=1, mode="promise_in_bounds")
                for places in picks[place // HALF]
            ]
            conds.append(parts[0])
            store[col, row] = parts[1]
            head[col, row] = parts[2]
            zone[col, row] = parts[3]
        for row, field in enumerate([up_sub(conds[-1])] + conds + [down_sub(conds[0])]):
            cond[col, row] = field


def coefficients(zone_base, cond, store, head, zone, keep, gain, source):
    wanted = (zone_base + lane_places() % GROUP).astype(jnp.float32)

    def column(col):
        sums = rows_sum([cond[col, row] for row in range(ROWS + 2)])
        return [layers_sum(field) for field in sums]

    def emit(col, around):
        keeps, gains, sources = [], [], []
        for row in range(ROWS):
            here = cond[col, row + 1]
            near = here * (0.25 * around[row])
            diag = store[col, row] + (near - 2.0 * here * here)
            active = jnp.where(here > 0.0, 1.0, 0.0)
            step = RELAX * (active / (diag + 1.0 - active))
            scaled = step * here * here
            keeps.append(1.0 - step * (store[col, row] + near))
            gains.append(0.25 * scaled)
            sources.append(jnp.where(zone[col, row] == wanted, scaled * head[col, row], 0.0))
        for target, fields in ((keep, keeps), (gain, gains), (source, sources)):
            for row, field in enumerate([up_sub(fields[-1])] + fields + [down_sub(fields[0])]):
                target[col, row] = field

    column_loop(1, WIDE - 2, column, emit)


def collect(me, mine, other, raw):
    for place in range(SUBX):
        piece = (mine if place % 2 == 0 else other)[pl.ds((place // 2) * BLOCK, BLOCK), :]
        raw[pl.ds(pl.multiple_of((me ^ place) * BLOCK, 8), BLOCK), :] = piece


def main_kernel(info, mine, other, out0, out2, out4, out6, out, raw, cond, store, head, zone, keep, gain, source, state, *buffers):
    collect(info[0], mine, other, raw)
    expand(info[1] & 1, raw, cond, store, head, zone)
    coefficients(info[0] * GROUP, cond, store, head, zone, keep, gain, source)
    has_left, has_right = info[1] > 0, info[2] > 0
    left_own = jnp.where(has_left, 0.5, 1.0)
    right_own = jnp.where(has_right, 0.5, 1.0)
    subs = sub_places()
    low_own = jnp.where(subs == 0, 1.0, 0.5)
    high_own = jnp.where(subs == SUBX - 1, 1.0, 0.5)
    high = HALO + COLS
    bases = (0, HALO - 2, high - 2)
    ends = (HALO + 1, high + 1, WIDE - 1)
    rims = ((HALO + 1,), (HALO - 2, high + 1), (high - 2,))
    fields = tuple((buffers[2 * k], buffers[2 * k + 1]) for k in range(3))
    zeros = jnp.zeros(TILE, jnp.float32)

    for outer in range(3):
        reach = 4 * (2 - outer)
        for part in range(3):
            for buffer in fields[part]:
                for col in rims[part]:
                    for row in range(6):
                        buffer[col - bases[part], row] = zeros if outer == 0 else state[col, row + 1]
        for sweep in range(4):
            more = reach + 3 - sweep
            ranges = (
                (HALO - more, HALO),
                (HALO - 1, high) if more > 0 else (HALO, high - 1),
                (high - 1, high - 1 + more),
            )
            for part in range(3):
                base = bases[part]
                old, new = fields[part][(sweep + 1) % 2], fields[part][sweep % 2]
                first, last = ranges[part]
                if outer == 0 and sweep == 0:
                    def copy(col, carry, new=new, base=base):
                        for row in range(6):
                            new[col - base, row] = source[col, row]
                        return carry
                    lax.fori_loop(first, last + 1, copy, 0, unroll=True)
                    continue

                def column(col, old=old, base=base, sweep=sweep, outer=outer):
                    if sweep == 0:
                        cells = [state[col, row] for row in range(8)]
                    else:
                        cells = [old[col - base, row] for row in range(6)]
                        if outer == 0:
                            cells = [None] + cells + [None]
                        else:
                            cells = [state[col, 0]] + cells + [state[col, 7]]
                    return [layers_sum(field) for field in rows_sum(cells)]

                def emit(col, around, old=old, new=new, base=base, sweep=sweep):
                    for row in range(6):
                        here = state[col, row + 1] if sweep == 0 else old[col - base, row]
                        new[col - base, row] = (
                            source[col, row] + keep[col, row] * here + gain[col, row] * around[row]
                        )

                column_loop(first, last, column, emit)

        done = tuple(fields[part][1] for part in range(3))

        def merge(col, cells, final):
            mine = [
                low_own * cells[1] + (1.0 - low_own) * pltpu.roll(cells[5], 1, 0),
                cells[2],
                cells[3],
                high_own * cells[4] + (1.0 - high_own) * pltpu.roll(cells[0], SUBX - 1, 0),
            ]
            if final:
                for row in range(ROWS):
                    here = cond[col, row + 1]
                    inside = here > 0.0
                    value = jnp.where(inside, mine[row] / jnp.where(inside, here, 1.0), 0.0)
                    out[pl.ds(row * COLS + col - HALO, SUBX, stride=ROWS * COLS), :] = value
            else:
                for row in range(ROWS):
                    state[col, row + 2] = mine[row]
                state[col, 0] = up_sub(mine[2])
                state[col, 1] = up_sub(mine[3])
                state[col, 6] = down_sub(mine[0])
                state[col, 7] = down_sub(mine[1])

        def merge_range(first, last, part):
            def body(col, carry):
                merge(col, [done[part][col - bases[part], row] for row in range(6)], outer == 2)
                return carry
            lax.fori_loop(first, last + 1, body, 0, unroll=True)

        def merge_mixed(col, part, own):
            cells = [
                own * done[1][col - bases[1], row] + (1.0 - own) * done[part][col - bases[part], row]
                for row in range(6)
            ]
            merge(col, cells, outer == 2)

        lefts = (HALO - 1, HALO) if outer < 2 else (HALO,)
        rights = (high - 1, high) if outer < 2 else (high - 1,)
        for col in lefts:
            merge_mixed(col, 0, left_own)
        for col in rights:
            merge_mixed(col, 2, right_own)
        merge_range(HALO + 1, high - 2, 1)
        if outer < 2:
            merge_range(HALO - reach, HALO - 2, 0)
            merge_range(high + 1, high - 1 + reach, 2)

    for place in range(SUBX):
        target = (out0, out2, out4, out6)[place // 2]
        chunk = out[pl.ds(pl.multiple_of((info[0] ^ place) * PLACES, 8), PLACES), :]
        target[(place % 2) * PLACES : (place % 2 + 1) * PLACES, :] = chunk


def run_main(info, mine, other):
    def cells(cols, rows):
        return pltpu.VMEM((cols, rows) + TILE, jnp.float32)

    scratch = [pltpu.VMEM((SUBX * rows, 128), jnp.float32) for rows in (PLACES, BLOCK)] + [cells(WIDE, 6)] + [cells(WIDE, ROWS)] * 3 + [cells(WIDE, 6)] * 3 + [cells(WIDE, 8)]
    scratch += [cells(HALO + 2, 6)] * 2 + [cells(COLS + 4, 6)] * 2 + [cells(HALO + 2, 6)] * 2
    return pl.pallas_call(
        main_kernel,
        out_shape=(jax.ShapeDtypeStruct((2 * PLACES, TILE[1]), jnp.float32),) * 4,
        in_specs=[pl.BlockSpec(memory_space=pltpu.SMEM)] + [pl.BlockSpec(memory_space=pltpu.VMEM)] * 2,
        out_specs=(pl.BlockSpec(memory_space=pltpu.VMEM),) * 4,
        scratch_shapes=scratch,
        compiler_params=pltpu.CompilerParams(vmem_limit_bytes=40 * 1024 * 1024),
        name="schwarz",
    )(info, mine, other)


def swap_blocks(fields):
    lanes = lane_places()
    width = 128 // SUBX
    fields = list(fields)
    for step in (1, 2, 4):
        late = (lanes // width) & step != 0
        for low in range(SUBX):
            if low & step:
                continue
            a, b = fields[low], fields[low | step]
            fields[low] = jnp.where(late, pltpu.roll(b, step * width, 1), a)
            fields[low | step] = jnp.where(late, b, pltpu.roll(a, 128 - step * width, 1))
    return fields


def place_kernel(info, index, own, got2, got4, got6, other, tangent, picks, parts, table):
    lanes = lane_places()
    for place in range(SUBX):
        near = (own, got2, got4, got6)[place // 2]
        if place % 2 == 0:
            chunk = near[0:PLACES, :]
        else:
            chunk = other[(place // 2) * PLACES : (place // 2 + 1) * PLACES, :]
        parts[pl.ds(pl.multiple_of((info[0] ^ place) * PLACES, 8), PLACES), :] = chunk
    order = (lanes % ZONES) // GROUP * 16 + lanes // ZONES * GROUP + lanes % GROUP
    entries = PLACES * LAYERS // 2
    for start in range(0, PLACES, 8):
        blocks = swap_blocks([parts[a * PLACES + start : a * PLACES + start + 8, :] for a in range(SUBX)])
        for pair in range(SUBX):
            whole = jnp.take_along_axis(blocks[pair], order, axis=1, mode="promise_in_bounds")
            tangent[start : start + 8, pair * 128 : (pair + 1) * 128] = whole
            line = pair * PLACES + start
            table[line : line + 8, :] = whole
            table[entries + line : entries + line + 8, :] = pltpu.roll(whole, ZONES, 1)
    table[2 * entries : 2 * entries + 8, :] = jnp.zeros(TILE, jnp.float32)
    upper = lax.broadcasted_iota(jnp.int32, (1, 128), 1) >= ZONES
    for owner in range(SUBY):
        for slot in range(CAP // 2):
            low = table[pl.ds(index[slot, owner], 1), :]
            high = table[pl.ds(index[slot + CAP // 2, owner], 1), :]
            line = owner * (CAP // 2) + slot
            picks[line : line + 1, :] = jnp.where(upper, high, low)


def run_place(info, index, *pieces):
    entries = PLACES * LAYERS // 2
    return pl.pallas_call(
        place_kernel,
        out_shape=(
            jax.ShapeDtypeStruct((PLACES, LAYERS * ZONES), jnp.float32),
            jax.ShapeDtypeStruct((SUBY * CAP // 2, 128), jnp.float32),
        ),
        in_specs=[pl.BlockSpec(memory_space=pltpu.SMEM)] * 2 + [pl.BlockSpec(memory_space=pltpu.VMEM)] * 5,
        out_specs=(pl.BlockSpec(memory_space=pltpu.VMEM),) * 2,
        scratch_shapes=[
            pltpu.VMEM((SUBX * PLACES, 128), jnp.float32),
            pltpu.VMEM((2 * entries + 8, 128), jnp.float32),
        ],
        name="place",
    )(info, index, *pieces)


def finish_kernel(arrived, wells):
    across = arrived[...].T
    lanes = lane_places()
    for start in range(0, ZONES, 8):
        low, high = across[start : start + 8], across[ZONES + start : ZONES + start + 8]
        for half in range(2):
            places = (half * 16 + lanes // CAP) * (CAP // 2) + lanes % (CAP // 2)
            both = [
                jnp.take_along_axis(part, places, axis=1, mode="promise_in_bounds") for part in (low, high)
            ]
            wells[start : start + 8, half * 128 : (half + 1) * 128] = jnp.where(
                lanes % CAP < CAP // 2, both[0], both[1]
            )


def run_finish(arrived):
    return pl.pallas_call(
        finish_kernel,
        out_shape=jax.ShapeDtypeStruct((ZONES, SUBY * CAP), jnp.float32),
        in_specs=[pl.BlockSpec(memory_space=pltpu.VMEM)],
        out_specs=pl.BlockSpec(memory_space=pltpu.VMEM),
        name="finish",
    )(arrived)


def swap(array, axis, pairs):
    return lax.ppermute(array, axis, pairs)


def partners(shift):
    return [(i, i ^ shift) for i in range(SUBX)]


def gather_inputs(conductivity, storage, head_term, zone_id, layer_count):
    own = run_pack(layer_count, conductivity, storage, head_term, zone_id)
    inner = [(i, i ^ 1) for i in range(SUBY)]
    outer = [(i, i + 1) for i in range(1, SUBY - 1, 2)]
    outer = outer + [(j, i) for i, j in outer]
    wide = jnp.concatenate([own, swap(own, "gy", inner), swap(own, "gy", outer)], axis=0)
    mine = jnp.concatenate([wide] + [swap(wide, "gx", partners(shift)) for shift in (2, 4, 6)], axis=0)
    return mine, swap(mine, "gx", partners(1))


def line_index(well_cell, well_count):
    cells = well_cell.T
    slots = jnp.arange(CAP, dtype=jnp.int32)[:, None]
    layer = cells & (LAYERS - 1)
    entries = PLACES * LAYERS // 2
    turned = (layer & 1) != (slots >= CAP // 2).astype(jnp.int32)
    lines = (layer >> 1) * PLACES + (cells >> 4) + jnp.where(turned, entries, 0)
    return jnp.where(slots < well_count[None, :], lines, 2 * entries)


def shards(conductivity, storage, head_term, zone_id, layer_count, well_cell, well_count):
    mine, other = gather_inputs(conductivity, storage, head_term, zone_id, layer_count)
    row, col = lax.axis_index("gx"), lax.axis_index("gy")
    info = jnp.stack([row, col, SUBY - 1 - col]).astype(jnp.int32)
    index = line_index(well_cell[0, 0], well_count[0, 0])
    sends = run_main(info, mine, other)
    near = [sends[0]] + [swap(sends[k], "gx", partners(2 * k)) for k in (1, 2, 3)]
    far = swap(jnp.concatenate([part[PLACES:] for part in near], axis=0), "gx", partners(1))
    tangent, picks = run_place(info, index, *near, far)
    picks = picks.reshape(SUBY, CAP // 2, 128)
    arrived = lax.all_to_all(picks, "gy", split_axis=0, concat_axis=0, tiled=True)
    wells = run_finish(arrived.reshape(SUBY * CAP // 2, 128)).T
    return (tangent.reshape(ROWS, COLS, LAYERS * ZONES), wells)


def solution(mesh):
    placed = (
        P("gx", "gy", None),
        P("gx", "gy", None),
        P("gx", "gy", None),
        P("gx", "gy", None),
        P("gx", "gy"),
        P("gx", "gy", None, None),
        P("gx", "gy", None),
    )
    return jax.shard_map(
        shards,
        mesh=mesh,
        in_specs=placed,
        out_specs=(P("gx", "gy", None), P(("gx", "gy"), None)),
        check_vma=False,
    )
```

```python
import jax
import jax.numpy as jnp
from jax import lax
from jax.experimental import pallas as pl
from jax.experimental.pallas import tpu as pltpu
from jax.sharding import PartitionSpec as P

ROWS, COLS, LAYERS, ZONES = 4, 16, 16, 64
HALO = 12
WIDE = COLS + 2 * HALO
HALF = COLS // 2
OWN = ROWS * HALF
BLOCK = 3 * OWN
PLACES = ROWS * COLS
SUBX, SUBY = 8, 32
CAP = 8
GROUP = ZONES // SUBX
TILE = (SUBX, LAYERS * GROUP)
RELAX = 0.8


def total(first, second):
    return first if second is None else second if first is None else first + second


def lane_places():
    return lax.broadcasted_iota(jnp.int32, TILE, 1)


def sub_places():
    return lax.broadcasted_iota(jnp.int32, TILE, 0)


def up_sub(field):
    return jnp.where(sub_places() == 0, 0.0, pltpu.roll(field, 1, 0))


def down_sub(field):
    return jnp.where(sub_places() == SUBX - 1, 0.0, pltpu.roll(field, SUBX - 1, 0))


def layers_sum(field):
    lanes = lane_places()
    above = jnp.where(lanes >= TILE[1] - GROUP, 0.0, pltpu.roll(field, TILE[1] - GROUP, 1))
    below = jnp.where(lanes < GROUP, 0.0, pltpu.roll(field, GROUP, 1))
    return (field + above) + (field + below)


def rows_sum(cells):
    pairs = [total(a, b) for a, b in zip(cells[:-1], cells[1:])]
    return [total(a, b) for a, b in zip(pairs[:-1], pairs[1:])]


def column_loop(first, last, column, emit):
    before = column(first - 1)
    here = column(first)
    pair = [a + b for a, b in zip(before, here)]

    def one(col, here, pair):
        after = column(col + 1)
        next_pair = [a + b for a, b in zip(here, after)]
        emit(col, [a + b for a, b in zip(pair, next_pair)])
        return after, next_pair

    for col in range(first, last + 1):
        here, pair = one(col, here, pair)


def pack_kernel(layers, conductivity, storage, head, zone, own):
    live = lax.broadcasted_iota(jnp.int32, (HALF, LAYERS), 1) < layers[0, 0]
    for row in range(ROWS):
        parts = []
        for half in range(2):
            cols = slice(half * HALF, (half + 1) * HALF)
            parts.append(jnp.where(live, jnp.sqrt(conductivity[row, cols, :]), 0.0))
            parts.append(storage[row, cols, :])
            parts.append(head[row, cols, :])
            parts.append(zone[row, cols, :].astype(jnp.float32))
        own[row * HALF : (row + 1) * HALF, :] = jnp.concatenate(parts, axis=1)


def run_pack(layers, conductivity, storage, head, zone):
    return pl.pallas_call(
        pack_kernel,
        out_shape=jax.ShapeDtypeStruct((OWN, 128), jnp.float32),
        in_specs=[pl.BlockSpec(memory_space=pltpu.SMEM)] + [pl.BlockSpec(memory_space=pltpu.VMEM)] * 4,
        out_specs=pl.BlockSpec(memory_space=pltpu.VMEM),
        compiler_params=pltpu.CompilerParams(vmem_limit_bytes=4 * 1024 * 1024),
        name="pack",
    )(layers, conductivity, storage, head, zone)


def expand(odd, raw, cond, store, head, zone):
    lanes = lane_places()
    picks = [[half * 64 + part * LAYERS + lanes // GROUP for part in range(4)] for half in range(2)]
    bases = (2 * OWN - odd * OWN, 0, OWN + odd * OWN)

    for col in range(WIDE):
        block, place = divmod(col - HALO + COLS, COLS)
        conds = []
        for row in range(ROWS):
            packed = raw[pl.ds(bases[block] + row * HALF + place % HALF, SUBX, stride=BLOCK), :]
            parts = [
                jnp.take_along_axis(packed, places, axis=1, mode="promise_in_bounds")
                for places in picks[place // HALF]
            ]
            conds.append(parts[0])
            store[col, row] = parts[1]
            head[col, row] = parts[2]
            zone[col, row] = parts[3]
        for row, field in enumerate([up_sub(conds[-1])] + conds + [down_sub(conds[0])]):
            cond[col, row] = field


def coefficients(zone_base, cond, store, head, zone, keep, gain, source):
    wanted = (zone_base + lane_places() % GROUP).astype(jnp.float32)

    def column(col):
        sums = rows_sum([cond[col, row] for row in range(ROWS + 2)])
        return [layers_sum(field) for field in sums]

    def emit(col, around):
        keeps, gains, sources = [], [], []
        for row in range(ROWS):
            here = cond[col, row + 1]
            near = here * (0.25 * around[row])
            diag = store[col, row] + (near - 2.0 * here * here)
            active = jnp.where(here > 0.0, 1.0, 0.0)
            step = RELAX * (active / (diag + 1.0 - active))
            scaled = step * here * here
            keeps.append(1.0 - step * (store[col, row] + near))
            gains.append(0.25 * scaled)
            sources.append(jnp.where(zone[col, row] == wanted, scaled * head[col, row], 0.0))
        for target, fields in ((keep, keeps), (gain, gains), (source, sources)):
            for row, field in enumerate([up_sub(fields[-1])] + fields + [down_sub(fields[0])]):
                target[col, row] = field

    column_loop(1, WIDE - 2, column, emit)


def collect(me, mine, other, raw):
    for place in range(SUBX):
        piece = (mine if place % 2 == 0 else other)[pl.ds((place // 2) * BLOCK, BLOCK), :]
        raw[pl.ds(pl.multiple_of((me ^ place) * BLOCK, 8), BLOCK), :] = piece


def main_kernel(info, mine, other, out0, out2, out4, out6, out, raw, cond, store, head, zone, keep, gain, source, state, *buffers):
    collect(info[0], mine, other, raw)
    expand(info[1] & 1, raw, cond, store, head, zone)
    coefficients(info[0] * GROUP, cond, store, head, zone, keep, gain, source)
    has_left, has_right = info[1] > 0, info[2] > 0
    left_own = jnp.where(has_left, 0.5, 1.0)
    right_own = jnp.where(has_right, 0.5, 1.0)
    subs = sub_places()
    low_own = jnp.where(subs == 0, 1.0, 0.5)
    high_own = jnp.where(subs == SUBX - 1, 1.0, 0.5)
    high = HALO + COLS
    bases = (0, HALO - 2, high - 2)
    ends = (HALO + 1, high + 1, WIDE - 1)
    rims = ((HALO + 1,), (HALO - 2, high + 1), (high - 2,))
    fields = tuple((buffers[2 * k], buffers[2 * k + 1]) for k in range(3))
    zeros = jnp.zeros(TILE, jnp.float32)

    for outer in range(3):
        reach = 4 * (2 - outer)
        for part in range(3):
            for buffer in fields[part]:
                for col in rims[part]:
                    for row in range(6):
                        buffer[col - bases[part], row] = zeros if outer == 0 else state[col, row + 1]
        for sweep in range(4):
            more = reach + 3 - sweep
            ranges = (
                (HALO - more, HALO),
                (HALO - 1, high) if more > 0 else (HALO, high - 1),
                (high - 1, high - 1 + more),
            )
            for part in range(3):
                base = bases[part]
                old, new = fields[part][(sweep + 1) % 2], fields[part][sweep % 2]
                first, last = ranges[part]
                if outer == 0 and sweep == 0:
                    def copy(col, carry, new=new, base=base):
                        for row in range(6):
                            new[col - base, row] = source[col, row]
                        return carry
                    lax.fori_loop(first, last + 1, copy, 0, unroll=True)
                    continue

                def column(col, old=old, base=base, sweep=sweep, outer=outer):
                    if sweep == 0:
                        cells = [state[col, row] for row in range(8)]
                    else:
                        cells = [old[col - base, row] for row in range(6)]
                        if outer == 0:
                            cells = [None] + cells + [None]
                        else:
                            cells = [state[col, 0]] + cells + [state[col, 7]]
                    return [layers_sum(field) for field in rows_sum(cells)]

                def emit(col, around, old=old, new=new, base=base, sweep=sweep):
                    for row in range(6):
                        here = state[col, row + 1] if sweep == 0 else old[col - base, row]
                        new[col - base, row] = (
                            source[col, row] + keep[col, row] * here + gain[col, row] * around[row]
                        )

                column_loop(first, last, column, emit)

        done = tuple(fields[part][1] for part in range(3))

        def merge(col, cells, final):
            mine = [
                low_own * cells[1] + (1.0 - low_own) * pltpu.roll(cells[5], 1, 0),
                cells[2],
                cells[3],
                high_own * cells[4] + (1.0 - high_own) * pltpu.roll(cells[0], SUBX - 1, 0),
            ]
            if final:
                for row in range(ROWS):
                    here = cond[col, row + 1]
                    inside = here > 0.0
                    value = jnp.where(inside, mine[row] / jnp.where(inside, here, 1.0), 0.0)
                    out[pl.ds(row * COLS + col - HALO, SUBX, stride=ROWS * COLS), :] = value
            else:
                for row in range(ROWS):
                    state[col, row + 2] = mine[row]
                state[col, 0] = up_sub(mine[2])
                state[col, 1] = up_sub(mine[3])
                state[col, 6] = down_sub(mine[0])
                state[col, 7] = down_sub(mine[1])

        def merge_range(first, last, part):
            def body(col, carry):
                merge(col, [done[part][col - bases[part], row] for row in range(6)], outer == 2)
                return carry
            lax.fori_loop(first, last + 1, body, 0, unroll=True)

        def merge_mixed(col, part, own):
            cells = [
                own * done[1][col - bases[1], row] + (1.0 - own) * done[part][col - bases[part], row]
                for row in range(6)
            ]
            merge(col, cells, outer == 2)

        lefts = (HALO - 1, HALO) if outer < 2 else (HALO,)
        rights = (high - 1, high) if outer < 2 else (high - 1,)
        for col in lefts:
            merge_mixed(col, 0, left_own)
        for col in rights:
            merge_mixed(col, 2, right_own)
        merge_range(HALO + 1, high - 2, 1)
        if outer < 2:
            merge_range(HALO - reach, HALO - 2, 0)
            merge_range(high + 1, high - 1 + reach, 2)

    for place in range(SUBX):
        target = (out0, out2, out4, out6)[place // 2]
        chunk = out[pl.ds(pl.multiple_of((info[0] ^ place) * PLACES, 8), PLACES), :]
        target[(place % 2) * PLACES : (place % 2 + 1) * PLACES, :] = chunk


def run_main(info, mine, other):
    def cells(cols, rows):
        return pltpu.VMEM((cols, rows) + TILE, jnp.float32)

    scratch = [pltpu.VMEM((SUBX * rows, 128), jnp.float32) for rows in (PLACES, BLOCK)] + [cells(WIDE, 6)] + [cells(WIDE, ROWS)] * 3 + [cells(WIDE, 6)] * 3 + [cells(WIDE, 8)]
    scratch += [cells(HALO + 2, 6)] * 2 + [cells(COLS + 4, 6)] * 2 + [cells(HALO + 2, 6)] * 2
    return pl.pallas_call(
        main_kernel,
        out_shape=(jax.ShapeDtypeStruct((2 * PLACES, TILE[1]), jnp.float32),) * 4,
        in_specs=[pl.BlockSpec(memory_space=pltpu.SMEM)] + [pl.BlockSpec(memory_space=pltpu.VMEM)] * 2,
        out_specs=(pl.BlockSpec(memory_space=pltpu.VMEM),) * 4,
        scratch_shapes=scratch,
        compiler_params=pltpu.CompilerParams(vmem_limit_bytes=40 * 1024 * 1024),
        name="schwarz",
    )(info, mine, other)


def swap_blocks(fields):
    lanes = lane_places()
    width = 128 // SUBX
    fields = list(fields)
    for step in (1, 2, 4):
        late = (lanes // width) & step != 0
        for low in range(SUBX):
            if low & step:
                continue
            a, b = fields[low], fields[low | step]
            fields[low] = jnp.where(late, pltpu.roll(b, step * width, 1), a)
            fields[low | step] = jnp.where(late, b, pltpu.roll(a, 128 - step * width, 1))
    return fields


def place_kernel(info, index, *refs):
    pieces, (tangent, picks, parts, table) = refs[:SUBX], refs[SUBX:]
    lanes = lane_places()
    for place in range(SUBX):
        side = place % 2
        chunk = pieces[side * 4 + place // 2][side * PLACES : (side + 1) * PLACES, :]
        parts[pl.ds(pl.multiple_of((info[0] ^ place) * PLACES, 8), PLACES), :] = chunk
    order = (lanes % ZONES) // GROUP * 16 + lanes // ZONES * GROUP + lanes % GROUP
    entries = PLACES * LAYERS // 2
    for start in range(0, PLACES, 8):
        blocks = swap_blocks([parts[a * PLACES + start : a * PLACES + start + 8, :] for a in range(SUBX)])
        for pair in range(SUBX):
            whole = jnp.take_along_axis(blocks[pair], order, axis=1, mode="promise_in_bounds")
            tangent[start : start + 8, pair * 128 : (pair + 1) * 128] = whole
            line = pair * PLACES + start
            table[line : line + 8, :] = whole
            table[entries + line : entries + line + 8, :] = pltpu.roll(whole, ZONES, 1)
    table[2 * entries : 2 * entries + 8, :] = jnp.zeros(TILE, jnp.float32)
    upper = lax.broadcasted_iota(jnp.int32, (1, 128), 1) >= ZONES
    for owner in range(SUBY):
        for slot in range(CAP // 2):
            low = table[pl.ds(index[slot, owner], 1), :]
            high = table[pl.ds(index[slot + CAP // 2, owner], 1), :]
            line = owner * (CAP // 2) + slot
            picks[line : line + 1, :] = jnp.where(upper, high, low)


def run_place(info, index, pieces):
    entries = PLACES * LAYERS // 2
    return pl.pallas_call(
        place_kernel,
        out_shape=(
            jax.ShapeDtypeStruct((PLACES, LAYERS * ZONES), jnp.float32),
            jax.ShapeDtypeStruct((SUBY * CAP // 2, 128), jnp.float32),
        ),
        in_specs=[pl.BlockSpec(memory_space=pltpu.SMEM)] * 2 + [pl.BlockSpec(memory_space=pltpu.VMEM)] * 8,
        out_specs=(pl.BlockSpec(memory_space=pltpu.VMEM),) * 2,
        scratch_shapes=[
            pltpu.VMEM((SUBX * PLACES, 128), jnp.float32),
            pltpu.VMEM((2 * entries + 8, 128), jnp.float32),
        ],
        compiler_params=pltpu.CompilerParams(vmem_limit_bytes=8 * 1024 * 1024),
        name="place",
    )(info, index, *pieces)


def finish_kernel(arrived, wells):
    across = arrived[...].T
    lanes = lane_places()
    for start in range(0, ZONES, 8):
        low, high = across[start : start + 8], across[ZONES + start : ZONES + start + 8]
        for half in range(2):
            places = (half * 16 + lanes // CAP) * (CAP // 2) + lanes % (CAP // 2)
            both = [
                jnp.take_along_axis(part, places, axis=1, mode="promise_in_bounds") for part in (low, high)
            ]
            wells[start : start + 8, half * 128 : (half + 1) * 128] = jnp.where(
                lanes % CAP < CAP // 2, both[0], both[1]
            )


def run_finish(arrived):
    return pl.pallas_call(
        finish_kernel,
        out_shape=jax.ShapeDtypeStruct((ZONES, SUBY * CAP), jnp.float32),
        in_specs=[pl.BlockSpec(memory_space=pltpu.VMEM)],
        out_specs=pl.BlockSpec(memory_space=pltpu.VMEM),
        compiler_params=pltpu.CompilerParams(vmem_limit_bytes=4 * 1024 * 1024),
        name="finish",
    )(arrived)


def swap(array, axis, pairs):
    return lax.ppermute(array, axis, pairs)


def partners(shift):
    return [(i, i ^ shift) for i in range(SUBX)]


def gather_inputs(conductivity, storage, head_term, zone_id, layer_count, others):
    own = run_pack(layer_count, conductivity, storage, head_term, zone_id)
    inner = [(i, i ^ 1) for i in range(SUBY)]
    outer = [(i, i + 1) for i in range(1, SUBY - 1, 2)]
    outer = outer + [(j, i) for i, j in outer]
    wide = jnp.concatenate([own, swap(own, "gy", inner), swap(own, "gy", outer)], axis=0)
    wide, others = lax.optimization_barrier((wide, others))
    mine = jnp.concatenate([wide] + [swap(wide, "gx", partners(shift)) for shift in (2, 4, 6)], axis=0)
    return mine, swap(mine, "gx", partners(1)), others


def line_index(well_cell, well_count):
    cells = well_cell.T
    slots = jnp.arange(CAP, dtype=jnp.int32)[:, None]
    layer = cells & (LAYERS - 1)
    entries = PLACES * LAYERS // 2
    turned = (layer & 1) != (slots >= CAP // 2).astype(jnp.int32)
    lines = (layer >> 1) * PLACES + (cells >> 4) + jnp.where(turned, entries, 0)
    return jnp.where(slots < well_count[None, :], lines, 2 * entries)


def shards(conductivity, storage, head_term, zone_id, layer_count, well_cell, well_count):
    row, col = lax.axis_index("gx"), lax.axis_index("gy")
    info = jnp.stack([row, col, SUBY - 1 - col]).astype(jnp.int32)
    index = line_index(well_cell[0, 0], well_count[0, 0])
    mine, other, (info, index) = gather_inputs(
        conductivity, storage, head_term, zone_id, layer_count, (info, index)
    )
    sends = run_main(info, mine, other)
    near = [sends[0]] + [swap(sends[k], "gx", partners(2 * k)) for k in (1, 2, 3)]
    far = [swap(part, "gx", partners(1)) for part in near]
    tangent, picks = run_place(info, index, near + far)
    picks = picks.reshape(SUBY, CAP // 2, 128)
    arrived = lax.all_to_all(picks, "gy", split_axis=0, concat_axis=0, tiled=True)
    wells = run_finish(arrived.reshape(SUBY * CAP // 2, 128)).T
    return (tangent.reshape(ROWS, COLS, LAYERS * ZONES), wells)


def solution(mesh):
    placed = (
        P("gx", "gy", None),
        P("gx", "gy", None),
        P("gx", "gy", None),
        P("gx", "gy", None),
        P("gx", "gy"),
        P("gx", "gy", None, None),
        P("gx", "gy", None),
    )
    return jax.shard_map(
        shards,
        mesh=mesh,
        in_specs=placed,
        out_specs=(P("gx", "gy", None), P(("gx", "gy"), None)),
        check_vma=False,
    )
```

```python
import jax
import jax.numpy as jnp
from jax import lax
from jax.experimental import pallas as pl
from jax.experimental.pallas import tpu as pltpu
from jax.sharding import PartitionSpec as P

ROWS, COLS, LAYERS, ZONES = 4, 16, 16, 64
HALO = 12
WIDE = COLS + 2 * HALO
HALF = COLS // 2
OWN = ROWS * HALF
BLOCK = 3 * OWN
PLACES = ROWS * COLS
SUBX, SUBY = 8, 32
CAP = 8
GROUP = ZONES // SUBX
TILE = (SUBX, LAYERS * GROUP)
RELAX = 0.8


def total(first, second):
    return first if second is None else second if first is None else first + second


def lane_places():
    return lax.broadcasted_iota(jnp.int32, TILE, 1)


def sub_places():
    return lax.broadcasted_iota(jnp.int32, TILE, 0)


def up_sub(field):
    return jnp.where(sub_places() == 0, 0.0, pltpu.roll(field, 1, 0))


def down_sub(field):
    return jnp.where(sub_places() == SUBX - 1, 0.0, pltpu.roll(field, SUBX - 1, 0))


def layers_sums(fields):
    lanes = lane_places()
    above = [pltpu.roll(field, TILE[1] - GROUP, 1) for field in fields]
    below = [pltpu.roll(field, GROUP, 1) for field in fields]
    return [
        (field + jnp.where(lanes >= TILE[1] - GROUP, 0.0, up)) + (field + jnp.where(lanes < GROUP, 0.0, down))
        for field, up, down in zip(fields, above, below)
    ]


def rows_sum(cells):
    pairs = [total(a, b) for a, b in zip(cells[:-1], cells[1:])]
    return [total(a, b) for a, b in zip(pairs[:-1], pairs[1:])]


def column_loop(first, last, column, emit):
    before = column(first - 1)
    here = column(first)
    pair = [a + b for a, b in zip(before, here)]

    def one(col, here, pair):
        after = column(col + 1)
        next_pair = [a + b for a, b in zip(here, after)]
        emit(col, [a + b for a, b in zip(pair, next_pair)])
        return after, next_pair

    for col in range(first, last + 1):
        here, pair = one(col, here, pair)


def pack_kernel(layers, conductivity, storage, head, zone, own):
    live = lax.broadcasted_iota(jnp.int32, (HALF, LAYERS), 1) < layers[0, 0]
    for row in range(ROWS):
        parts = []
        for half in range(2):
            cols = slice(half * HALF, (half + 1) * HALF)
            parts.append(jnp.where(live, jnp.sqrt(conductivity[row, cols, :]), 0.0))
            parts.append(storage[row, cols, :])
            parts.append(head[row, cols, :])
            parts.append(zone[row, cols, :].astype(jnp.float32))
        own[row * HALF : (row + 1) * HALF, :] = jnp.concatenate(parts, axis=1)


def run_pack(layers, conductivity, storage, head, zone):
    return pl.pallas_call(
        pack_kernel,
        out_shape=jax.ShapeDtypeStruct((OWN, 128), jnp.float32),
        in_specs=[pl.BlockSpec(memory_space=pltpu.SMEM)] + [pl.BlockSpec(memory_space=pltpu.VMEM)] * 4,
        out_specs=pl.BlockSpec(memory_space=pltpu.VMEM),
        compiler_params=pltpu.CompilerParams(vmem_limit_bytes=4 * 1024 * 1024),
        name="pack",
    )(layers, conductivity, storage, head, zone)


def expand(odd, raw, cond, store, head, zone):
    lanes = lane_places()
    picks = [[half * 64 + part * LAYERS + lanes // GROUP for part in range(4)] for half in range(2)]
    bases = (2 * OWN - odd * OWN, 0, OWN + odd * OWN)

    for half in range(2):
        for part, target in enumerate((cond, store, head, zone)):
            for col in range(WIDE):
                block, place = divmod(col - HALO + COLS, COLS)
                if place // HALF != half:
                    continue
                for row in range(ROWS):
                    packed = raw[pl.ds(bases[block] + row * HALF + place % HALF, SUBX, stride=BLOCK), :]
                    target[col, row + (part == 0)] = jnp.take_along_axis(
                        packed, picks[half][part], axis=1, mode="promise_in_bounds"
                    )
    for col in range(WIDE):
        cond[col, 0] = up_sub(cond[col, ROWS])
        cond[col, ROWS + 1] = down_sub(cond[col, 1])


def coefficients(zone_base, cond, store, head, zone, keep, gain, source):
    wanted = (zone_base + lane_places() % GROUP).astype(jnp.float32)

    def column(col):
        sums = rows_sum([cond[col, row] for row in range(ROWS + 2)])
        return layers_sums(sums)

    def emit(col, around):
        keeps, gains, sources = [], [], []
        for row in range(ROWS):
            here = cond[col, row + 1]
            near = here * (0.25 * around[row])
            diag = store[col, row] + (near - 2.0 * here * here)
            active = jnp.where(here > 0.0, 1.0, 0.0)
            step = RELAX * (active / (diag + 1.0 - active))
            scaled = step * here * here
            keeps.append(1.0 - step * (store[col, row] + near))
            gains.append(0.25 * scaled)
            sources.append(jnp.where(zone[col, row] == wanted, scaled * head[col, row], 0.0))
        for target, fields in ((keep, keeps), (gain, gains), (source, sources)):
            for row, field in enumerate([up_sub(fields[-1])] + fields + [down_sub(fields[0])]):
                target[col, row] = field

    column_loop(1, WIDE - 2, column, emit)


def collect(me, mine, other, raw):
    for place in range(SUBX):
        piece = (mine if place % 2 == 0 else other)[pl.ds((place // 2) * BLOCK, BLOCK), :]
        raw[pl.ds(pl.multiple_of((me ^ place) * BLOCK, 8), BLOCK), :] = piece


def main_kernel(info, mine, other, out0, out2, out4, out6, out, raw, cond, store, head, zone, keep, gain, source, state, *buffers):
    collect(info[0], mine, other, raw)
    expand(info[1] & 1, raw, cond, store, head, zone)
    coefficients(info[0] * GROUP, cond, store, head, zone, keep, gain, source)
    has_left, has_right = info[1] > 0, info[2] > 0
    left_own = jnp.where(has_left, 0.5, 1.0)
    right_own = jnp.where(has_right, 0.5, 1.0)
    subs = sub_places()
    low_own = jnp.where(subs == 0, 1.0, 0.5)
    high_own = jnp.where(subs == SUBX - 1, 1.0, 0.5)
    high = HALO + COLS
    bases = (0, HALO - 2, high - 2)
    ends = (HALO + 1, high + 1, WIDE - 1)
    rims = ((HALO + 1,), (HALO - 2, high + 1), (high - 2,))
    fields = tuple((buffers[2 * k], buffers[2 * k + 1]) for k in range(3))
    zeros = jnp.zeros(TILE, jnp.float32)

    for outer in range(3):
        reach = 4 * (2 - outer)
        for part in range(3):
            for buffer in fields[part]:
                for col in rims[part]:
                    for row in range(6):
                        buffer[col - bases[part], row] = zeros if outer == 0 else state[col, row + 1]
        for sweep in range(4):
            more = reach + 3 - sweep
            ranges = (
                (HALO - more, HALO),
                (HALO - 1, high) if more > 0 else (HALO, high - 1),
                (high - 1, high - 1 + more),
            )
            for part in range(3):
                base = bases[part]
                old, new = fields[part][(sweep + 1) % 2], fields[part][sweep % 2]
                first, last = ranges[part]
                if outer == 0 and sweep == 0:
                    continue
                begun = outer == 0 and sweep == 1

                def column(col, old=old, base=base, sweep=sweep, outer=outer, begun=begun, rim=rims[part]):
                    if begun and col in rim:
                        return [zeros] * 6
                    if begun:
                        cells = [None] + [source[col, row] for row in range(6)] + [None]
                    elif sweep == 0:
                        cells = [state[col, row] for row in range(8)]
                    else:
                        cells = [old[col - base, row] for row in range(6)]
                        if outer == 0:
                            cells = [None] + cells + [None]
                        else:
                            cells = [state[col, 0]] + cells + [state[col, 7]]
                    return layers_sums(rows_sum(cells))

                def emit(col, around, old=old, new=new, base=base, sweep=sweep, begun=begun):
                    for row in range(6):
                        if begun:
                            here = source[col, row]
                        else:
                            here = state[col, row + 1] if sweep == 0 else old[col - base, row]
                        new[col - base, row] = (
                            source[col, row] + keep[col, row] * here + gain[col, row] * around[row]
                        )

                column_loop(first, last, column, emit)

        done = tuple(fields[part][1] for part in range(3))

        def merge(col, cells, final):
            mine = [
                low_own * cells[1] + (1.0 - low_own) * pltpu.roll(cells[5], 1, 0),
                cells[2],
                cells[3],
                high_own * cells[4] + (1.0 - high_own) * pltpu.roll(cells[0], SUBX - 1, 0),
            ]
            if final:
                for row in range(ROWS):
                    here = cond[col, row + 1]
                    inside = here > 0.0
                    value = jnp.where(inside, mine[row] / jnp.where(inside, here, 1.0), 0.0)
                    out[pl.ds(row * COLS + col - HALO, SUBX, stride=ROWS * COLS), :] = value
            else:
                for row in range(ROWS):
                    state[col, row + 2] = mine[row]
                state[col, 0] = up_sub(mine[2])
                state[col, 1] = up_sub(mine[3])
                state[col, 6] = down_sub(mine[0])
                state[col, 7] = down_sub(mine[1])

        def merge_range(first, last, part):
            def body(col, carry):
                merge(col, [done[part][col - bases[part], row] for row in range(6)], outer == 2)
                return carry
            lax.fori_loop(first, last + 1, body, 0, unroll=True)

        def merge_mixed(col, part, own):
            cells = [
                own * done[1][col - bases[1], row] + (1.0 - own) * done[part][col - bases[part], row]
                for row in range(6)
            ]
            merge(col, cells, outer == 2)

        lefts = (HALO - 1, HALO) if outer < 2 else (HALO,)
        rights = (high - 1, high) if outer < 2 else (high - 1,)
        for col in lefts:
            merge_mixed(col, 0, left_own)
        for col in rights:
            merge_mixed(col, 2, right_own)
        merge_range(HALO + 1, high - 2, 1)
        if outer < 2:
            merge_range(HALO - reach, HALO - 2, 0)
            merge_range(high + 1, high - 1 + reach, 2)

    for place in range(SUBX):
        target = (out0, out2, out4, out6)[place // 2]
        chunk = out[pl.ds(pl.multiple_of((info[0] ^ place) * PLACES, 8), PLACES), :]
        target[(place % 2) * PLACES : (place % 2 + 1) * PLACES, :] = chunk


def run_main(info, mine, other):
    def cells(cols, rows):
        return pltpu.VMEM((cols, rows) + TILE, jnp.float32)

    scratch = [pltpu.VMEM((SUBX * rows, 128), jnp.float32) for rows in (PLACES, BLOCK)] + [cells(WIDE, 6)] + [cells(WIDE, ROWS)] * 3 + [cells(WIDE, 6)] * 3 + [cells(WIDE, 8)]
    scratch += [cells(HALO + 2, 6)] * 2 + [cells(COLS + 4, 6)] * 2 + [cells(HALO + 2, 6)] * 2
    return pl.pallas_call(
        main_kernel,
        out_shape=(jax.ShapeDtypeStruct((2 * PLACES, TILE[1]), jnp.float32),) * 4,
        in_specs=[pl.BlockSpec(memory_space=pltpu.SMEM)] + [pl.BlockSpec(memory_space=pltpu.VMEM)] * 2,
        out_specs=(pl.BlockSpec(memory_space=pltpu.VMEM),) * 4,
        scratch_shapes=scratch,
        compiler_params=pltpu.CompilerParams(vmem_limit_bytes=40 * 1024 * 1024),
        name="schwarz",
    )(info, mine, other)


def swap_blocks(fields):
    lanes = lane_places()
    width = 128 // SUBX
    fields = list(fields)
    for step in (1, 2, 4):
        late = (lanes // width) & step != 0
        for low in range(SUBX):
            if low & step:
                continue
            a, b = fields[low], fields[low | step]
            fields[low] = jnp.where(late, pltpu.roll(b, step * width, 1), a)
            fields[low | step] = jnp.where(late, b, pltpu.roll(a, 128 - step * width, 1))
    return fields


def place_kernel(info, index, near, far, tangent, picks, parts, table):
    lanes = lane_places()
    for place in range(SUBX):
        side = place % 2
        start = (2 * (3 - place // 2) + side) * PLACES
        chunk = (near, far)[side][start : start + PLACES, :]
        parts[pl.ds(pl.multiple_of((info[0] ^ place) * PLACES, 8), PLACES), :] = chunk
    order = (lanes % ZONES) // GROUP * 16 + lanes // ZONES * GROUP + lanes % GROUP
    entries = PLACES * LAYERS // 2
    for start in range(0, PLACES, 8):
        blocks = swap_blocks([parts[a * PLACES + start : a * PLACES + start + 8, :] for a in range(SUBX)])
        for pair in range(SUBX):
            whole = jnp.take_along_axis(blocks[pair], order, axis=1, mode="promise_in_bounds")
            tangent[start : start + 8, pair * 128 : (pair + 1) * 128] = whole
            line = pair * PLACES + start
            table[line : line + 8, :] = whole
            table[entries + line : entries + line + 8, :] = pltpu.roll(whole, ZONES, 1)
    table[2 * entries : 2 * entries + 8, :] = jnp.zeros(TILE, jnp.float32)
    upper = lax.broadcasted_iota(jnp.int32, (1, 128), 1) >= ZONES
    for owner in range(SUBY):
        for slot in range(CAP // 2):
            low = table[pl.ds(index[slot, owner], 1), :]
            high = table[pl.ds(index[slot + CAP // 2, owner], 1), :]
            line = owner * (CAP // 2) + slot
            picks[line : line + 1, :] = jnp.where(upper, high, low)


def run_place(info, index, pieces):
    entries = PLACES * LAYERS // 2
    return pl.pallas_call(
        place_kernel,
        out_shape=(
            jax.ShapeDtypeStruct((PLACES, LAYERS * ZONES), jnp.float32),
            jax.ShapeDtypeStruct((SUBY * CAP // 2, 128), jnp.float32),
        ),
        in_specs=[pl.BlockSpec(memory_space=pltpu.SMEM)] * 2 + [pl.BlockSpec(memory_space=pltpu.VMEM)] * 2,
        out_specs=(pl.BlockSpec(memory_space=pltpu.VMEM),) * 2,
        scratch_shapes=[
            pltpu.VMEM((SUBX * PLACES, 128), jnp.float32),
            pltpu.VMEM((2 * entries + 8, 128), jnp.float32),
        ],
        compiler_params=pltpu.CompilerParams(vmem_limit_bytes=8 * 1024 * 1024),
        name="place",
    )(info, index, *pieces)


def finish_kernel(arrived, wells):
    across = arrived[...].T
    lanes = lane_places()
    for start in range(0, ZONES, 8):
        low, high = across[start : start + 8], across[ZONES + start : ZONES + start + 8]
        for half in range(2):
            places = (half * 16 + lanes // CAP) * (CAP // 2) + lanes % (CAP // 2)
            both = [
                jnp.take_along_axis(part, places, axis=1, mode="promise_in_bounds") for part in (low, high)
            ]
            wells[start : start + 8, half * 128 : (half + 1) * 128] = jnp.where(
                lanes % CAP < CAP // 2, both[0], both[1]
            )


def run_finish(arrived):
    return pl.pallas_call(
        finish_kernel,
        out_shape=jax.ShapeDtypeStruct((ZONES, SUBY * CAP), jnp.float32),
        in_specs=[pl.BlockSpec(memory_space=pltpu.VMEM)],
        out_specs=pl.BlockSpec(memory_space=pltpu.VMEM),
        compiler_params=pltpu.CompilerParams(vmem_limit_bytes=4 * 1024 * 1024),
        name="finish",
    )(arrived)


def swap(array, axis, pairs):
    return lax.ppermute(array, axis, pairs)


def partners(shift):
    return [(i, i ^ shift) for i in range(SUBX)]


def gather_inputs(conductivity, storage, head_term, zone_id, layer_count, others):
    own = run_pack(layer_count, conductivity, storage, head_term, zone_id)
    inner = [(i, i ^ 1) for i in range(SUBY)]
    outer = [(i, i + 1) for i in range(1, SUBY - 1, 2)]
    outer = outer + [(j, i) for i, j in outer]
    wide = jnp.concatenate([own, swap(own, "gy", inner), swap(own, "gy", outer)], axis=0)
    wide, others = lax.optimization_barrier((wide, others))
    mine = jnp.concatenate([wide] + [swap(wide, "gx", partners(shift)) for shift in (2, 4, 6)], axis=0)
    return mine, swap(mine, "gx", partners(1)), others


def line_index(well_cell, well_count):
    cells = well_cell.T
    slots = jnp.arange(CAP, dtype=jnp.int32)[:, None]
    layer = cells & (LAYERS - 1)
    entries = PLACES * LAYERS // 2
    turned = (layer & 1) != (slots >= CAP // 2).astype(jnp.int32)
    lines = (layer >> 1) * PLACES + (cells >> 4) + jnp.where(turned, entries, 0)
    return jnp.where(slots < well_count[None, :], lines, 2 * entries)


def shards(conductivity, storage, head_term, zone_id, layer_count, well_cell, well_count):
    row, col = lax.axis_index("gx"), lax.axis_index("gy")
    info = jnp.stack([row, col, SUBY - 1 - col]).astype(jnp.int32)
    index = line_index(well_cell[0, 0], well_count[0, 0])
    mine, other, (info, index) = gather_inputs(
        conductivity, storage, head_term, zone_id, layer_count, (info, index)
    )
    sends = run_main(info, mine, other)
    near = [sends[0]] + [swap(sends[k], "gx", partners(2 * k)) for k in (1, 2, 3)]
    near = jnp.concatenate(near[::-1], axis=0)
    tangent, picks = run_place(info, index, (near, swap(near, "gx", partners(1))))
    picks = picks.reshape(SUBY, CAP // 2, 128)
    arrived = lax.all_to_all(picks, "gy", split_axis=0, concat_axis=0, tiled=True)
    wells = run_finish(arrived.reshape(SUBY * CAP // 2, 128)).T
    return (tangent.reshape(ROWS, COLS, LAYERS * ZONES), wells)


def solution(mesh):
    placed = (
        P("gx", "gy", None),
        P("gx", "gy", None),
        P("gx", "gy", None),
        P("gx", "gy", None),
        P("gx", "gy"),
        P("gx", "gy", None, None),
        P("gx", "gy", None),
    )
    return jax.shard_map(
        shards,
        mesh=mesh,
        in_specs=placed,
        out_specs=(P("gx", "gy", None), P(("gx", "gy"), None)),
        check_vma=False,
    )
```

```python
import jax
import jax.numpy as jnp
from jax import lax
from jax.experimental import pallas as pl
from jax.experimental.pallas import tpu as pltpu
from jax.sharding import PartitionSpec as P

ROWS, COLS, LAYERS, ZONES = 4, 16, 16, 64
HALO = 12
WIDE = COLS + 2 * HALO
HALF = COLS // 2
OWN = ROWS * HALF
BLOCK = 3 * OWN
PLACES = ROWS * COLS
SUBX, SUBY = 8, 32
CAP = 8
GROUP = ZONES // SUBX
TILE = (SUBX, LAYERS * GROUP)
RELAX = 0.8


def total(first, second):
    return first if second is None else second if first is None else first + second


def lane_places():
    return lax.broadcasted_iota(jnp.int32, TILE, 1)


def sub_places():
    return lax.broadcasted_iota(jnp.int32, TILE, 0)


def up_sub(field):
    return jnp.where(sub_places() == 0, 0.0, pltpu.roll(field, 1, 0))


def down_sub(field):
    return jnp.where(sub_places() == SUBX - 1, 0.0, pltpu.roll(field, SUBX - 1, 0))


def layers_sums(fields):
    lanes = lane_places()
    above = [pltpu.roll(field, TILE[1] - GROUP, 1) for field in fields]
    below = [pltpu.roll(field, GROUP, 1) for field in fields]
    return [
        (field + jnp.where(lanes >= TILE[1] - GROUP, 0.0, up)) + (field + jnp.where(lanes < GROUP, 0.0, down))
        for field, up, down in zip(fields, above, below)
    ]


def rows_sum(cells):
    pairs = [total(a, b) for a, b in zip(cells[:-1], cells[1:])]
    return [total(a, b) for a, b in zip(pairs[:-1], pairs[1:])]


def column_loop(first, last, column, emit):
    before = column(first - 1)
    here = column(first)
    pair = [a + b for a, b in zip(before, here)]

    def one(col, here, pair):
        after = column(col + 1)
        next_pair = [a + b for a, b in zip(here, after)]
        emit(col, [a + b for a, b in zip(pair, next_pair)])
        return after, next_pair

    for col in range(first, last + 1):
        here, pair = one(col, here, pair)


def pack_kernel(layers, conductivity, storage, head, zone, own):
    live = lax.broadcasted_iota(jnp.int32, (HALF, LAYERS), 1) < layers[0, 0]
    for row in range(ROWS):
        parts = []
        for half in range(2):
            cols = slice(half * HALF, (half + 1) * HALF)
            parts.append(jnp.where(live, jnp.sqrt(conductivity[row, cols, :]), 0.0))
            parts.append(storage[row, cols, :])
            parts.append(head[row, cols, :])
            parts.append(zone[row, cols, :].astype(jnp.float32))
        own[row * HALF : (row + 1) * HALF, :] = jnp.concatenate(parts, axis=1)


def run_pack(layers, conductivity, storage, head, zone):
    return pl.pallas_call(
        pack_kernel,
        out_shape=jax.ShapeDtypeStruct((OWN, 128), jnp.float32),
        in_specs=[pl.BlockSpec(memory_space=pltpu.SMEM)] + [pl.BlockSpec(memory_space=pltpu.VMEM)] * 4,
        out_specs=pl.BlockSpec(memory_space=pltpu.VMEM),
        compiler_params=pltpu.CompilerParams(vmem_limit_bytes=4 * 1024 * 1024),
        name="pack",
    )(layers, conductivity, storage, head, zone)


def expand(raw, cond, store, head, zone):
    lanes = lane_places()
    picks = [[half * 64 + part * LAYERS + lanes // GROUP for part in range(4)] for half in range(2)]
    bases = (OWN, 0, 2 * OWN)

    for half in range(2):
        for part, target in enumerate((cond, store, head, zone)):
            for col in range(WIDE):
                block, place = divmod(col - HALO + COLS, COLS)
                if place // HALF != half:
                    continue
                for row in range(ROWS):
                    packed = raw[pl.ds(bases[block] + row * HALF + place % HALF, SUBX, stride=BLOCK), :]
                    target[col, row + (part == 0)] = jnp.take_along_axis(
                        packed, picks[half][part], axis=1, mode="promise_in_bounds"
                    )
    for col in range(WIDE):
        cond[col, 0] = up_sub(cond[col, ROWS])
        cond[col, ROWS + 1] = down_sub(cond[col, 1])


def coefficients(zone_base, cond, store, head, zone, keep, gain, source):
    wanted = (zone_base + lane_places() % GROUP).astype(jnp.float32)

    def column(col):
        sums = rows_sum([cond[col, row] for row in range(ROWS + 2)])
        return layers_sums(sums)

    def emit(col, around):
        keeps, gains, sources = [], [], []
        for row in range(ROWS):
            here = cond[col, row + 1]
            near = here * (0.25 * around[row])
            diag = store[col, row] + (near - 2.0 * here * here)
            active = jnp.where(here > 0.0, 1.0, 0.0)
            step = RELAX * (active / (diag + 1.0 - active))
            scaled = step * here * here
            keeps.append(1.0 - step * (store[col, row] + near))
            gains.append(0.25 * scaled)
            sources.append(jnp.where(zone[col, row] == wanted, scaled * head[col, row], 0.0))
        for target, fields in ((keep, keeps), (gain, gains), (source, sources)):
            for row, field in enumerate([up_sub(fields[-1])] + fields + [down_sub(fields[0])]):
                target[col, row] = field

    column_loop(1, WIDE - 2, column, emit)


def collect(me, odd, mine, other, raw):
    for place in range(SUBX):
        for part, shift in enumerate((0, 2 * OWN - odd * OWN, OWN + odd * OWN)):
            start = (place // 2) * BLOCK + part * OWN
            piece = (mine if place % 2 == 0 else other)[start : start + OWN, :]
            raw[pl.ds(pl.multiple_of((me ^ place) * BLOCK + shift, 8), OWN), :] = piece


def main_kernel(info, mine, other, out0, out2, out4, out6, out, raw, cond, store, head, zone, keep, gain, source, state, *buffers):
    collect(info[0], info[1] & 1, mine, other, raw)
    expand(raw, cond, store, head, zone)
    coefficients(info[0] * GROUP, cond, store, head, zone, keep, gain, source)
    has_left, has_right = info[1] > 0, info[2] > 0
    left_own = jnp.where(has_left, 0.5, 1.0)
    right_own = jnp.where(has_right, 0.5, 1.0)
    subs = sub_places()
    low_own = jnp.where(subs == 0, 1.0, 0.5)
    high_own = jnp.where(subs == SUBX - 1, 1.0, 0.5)
    high = HALO + COLS
    bases = (0, HALO - 2, high - 2)
    ends = (HALO + 1, high + 1, WIDE - 1)
    rims = ((HALO + 1,), (HALO - 2, high + 1), (high - 2,))
    fields = tuple((buffers[2 * k], buffers[2 * k + 1]) for k in range(3))
    zeros = jnp.zeros(TILE, jnp.float32)

    for outer in range(3):
        reach = 4 * (2 - outer)
        for part in range(3):
            for buffer in fields[part]:
                for col in rims[part]:
                    for row in range(6):
                        buffer[col - bases[part], row] = zeros if outer == 0 else state[col, row + 1]
        for sweep in range(4):
            more = reach + 3 - sweep
            ranges = (
                (HALO - more, HALO),
                (HALO - 1, high) if more > 0 else (HALO, high - 1),
                (high - 1, high - 1 + more),
            )
            for part in range(3):
                base = bases[part]
                old, new = fields[part][(sweep + 1) % 2], fields[part][sweep % 2]
                first, last = ranges[part]
                if outer == 0 and sweep == 0:
                    continue
                begun = outer == 0 and sweep == 1

                def column(col, old=old, base=base, sweep=sweep, outer=outer, begun=begun, rim=rims[part]):
                    if begun and col in rim:
                        return [zeros] * 6
                    if begun:
                        cells = [None] + [source[col, row] for row in range(6)] + [None]
                    elif sweep == 0:
                        cells = [state[col, row] for row in range(8)]
                    else:
                        cells = [old[col - base, row] for row in range(6)]
                        if outer == 0:
                            cells = [None] + cells + [None]
                        else:
                            cells = [state[col, 0]] + cells + [state[col, 7]]
                    return layers_sums(rows_sum(cells))

                def emit(col, around, old=old, new=new, base=base, sweep=sweep, begun=begun):
                    for row in range(6):
                        if begun:
                            here = source[col, row]
                        else:
                            here = state[col, row + 1] if sweep == 0 else old[col - base, row]
                        new[col - base, row] = (
                            source[col, row] + keep[col, row] * here + gain[col, row] * around[row]
                        )

                column_loop(first, last, column, emit)

        done = tuple(fields[part][1] for part in range(3))

        def merge(col, cells, final):
            mine = [
                low_own * cells[1] + (1.0 - low_own) * pltpu.roll(cells[5], 1, 0),
                cells[2],
                cells[3],
                high_own * cells[4] + (1.0 - high_own) * pltpu.roll(cells[0], SUBX - 1, 0),
            ]
            if final:
                for row in range(ROWS):
                    here = cond[col, row + 1]
                    inside = here > 0.0
                    value = jnp.where(inside, mine[row] / jnp.where(inside, here, 1.0), 0.0)
                    out[pl.ds(row * COLS + col - HALO, SUBX, stride=ROWS * COLS), :] = value
            else:
                for row in range(ROWS):
                    state[col, row + 2] = mine[row]
                state[col, 0] = up_sub(mine[2])
                state[col, 1] = up_sub(mine[3])
                state[col, 6] = down_sub(mine[0])
                state[col, 7] = down_sub(mine[1])

        def merge_range(first, last, part):
            def body(col, carry):
                merge(col, [done[part][col - bases[part], row] for row in range(6)], outer == 2)
                return carry
            lax.fori_loop(first, last + 1, body, 0, unroll=True)

        def merge_mixed(col, part, own):
            cells = [
                own * done[1][col - bases[1], row] + (1.0 - own) * done[part][col - bases[part], row]
                for row in range(6)
            ]
            merge(col, cells, outer == 2)

        lefts = (HALO - 1, HALO) if outer < 2 else (HALO,)
        rights = (high - 1, high) if outer < 2 else (high - 1,)
        for col in lefts:
            merge_mixed(col, 0, left_own)
        for col in rights:
            merge_mixed(col, 2, right_own)
        merge_range(HALO + 1, high - 2, 1)
        if outer < 2:
            merge_range(HALO - reach, HALO - 2, 0)
            merge_range(high + 1, high - 1 + reach, 2)

    for place in range(SUBX):
        target = (out0, out2, out4, out6)[place // 2]
        chunk = out[pl.ds(pl.multiple_of((info[0] ^ place) * PLACES, 8), PLACES), :]
        target[(place % 2) * PLACES : (place % 2 + 1) * PLACES, :] = chunk


def run_main(info, mine, other):
    def cells(cols, rows):
        return pltpu.VMEM((cols, rows) + TILE, jnp.float32)

    scratch = [pltpu.VMEM((SUBX * rows, 128), jnp.float32) for rows in (PLACES, BLOCK)] + [cells(WIDE, 6)] + [cells(WIDE, ROWS)] * 3 + [cells(WIDE, 6)] * 3 + [cells(WIDE, 8)]
    scratch += [cells(HALO + 2, 6)] * 2 + [cells(COLS + 4, 6)] * 2 + [cells(HALO + 2, 6)] * 2
    return pl.pallas_call(
        main_kernel,
        out_shape=(jax.ShapeDtypeStruct((2 * PLACES, TILE[1]), jnp.float32),) * 4,
        in_specs=[pl.BlockSpec(memory_space=pltpu.SMEM)] + [pl.BlockSpec(memory_space=pltpu.VMEM)] * 2,
        out_specs=(pl.BlockSpec(memory_space=pltpu.VMEM),) * 4,
        scratch_shapes=scratch,
        compiler_params=pltpu.CompilerParams(vmem_limit_bytes=40 * 1024 * 1024),
        name="schwarz",
    )(info, mine, other)


def swap_blocks(fields):
    lanes = lane_places()
    width = 128 // SUBX
    fields = list(fields)
    for step in (1, 2, 4):
        late = (lanes // width) & step != 0
        for low in range(SUBX):
            if low & step:
                continue
            a, b = fields[low], fields[low | step]
            fields[low] = jnp.where(late, pltpu.roll(b, step * width, 1), a)
            fields[low | step] = jnp.where(late, b, pltpu.roll(a, 128 - step * width, 1))
    return fields


def place_kernel(info, index, near, far, tangent, picks, parts, table):
    lanes = lane_places()
    for place in range(SUBX):
        side = place % 2
        start = (2 * (3 - place // 2) + side) * PLACES
        chunk = (near, far)[side][start : start + PLACES, :]
        parts[pl.ds(pl.multiple_of((info[0] ^ place) * PLACES, 8), PLACES), :] = chunk
    order = (lanes % ZONES) // GROUP * 16 + lanes // ZONES * GROUP + lanes % GROUP
    entries = PLACES * LAYERS // 2
    for start in range(0, PLACES, 8):
        blocks = swap_blocks([parts[a * PLACES + start : a * PLACES + start + 8, :] for a in range(SUBX)])
        for pair in range(SUBX):
            whole = jnp.take_along_axis(blocks[pair], order, axis=1, mode="promise_in_bounds")
            tangent[start : start + 8, pair * 128 : (pair + 1) * 128] = whole
            line = pair * PLACES + start
            table[line : line + 8, :] = whole
            table[entries + line : entries + line + 8, :] = pltpu.roll(whole, ZONES, 1)
    table[2 * entries : 2 * entries + 8, :] = jnp.zeros(TILE, jnp.float32)
    upper = lax.broadcasted_iota(jnp.int32, (1, 128), 1) >= ZONES
    for owner in range(SUBY):
        for slot in range(CAP // 2):
            low = table[pl.ds(index[slot, owner], 1), :]
            high = table[pl.ds(index[slot + CAP // 2, owner], 1), :]
            line = owner * (CAP // 2) + slot
            picks[line : line + 1, :] = jnp.where(upper, high, low)


def run_place(info, index, pieces):
    entries = PLACES * LAYERS // 2
    return pl.pallas_call(
        place_kernel,
        out_shape=(
            jax.ShapeDtypeStruct((PLACES, LAYERS * ZONES), jnp.float32),
            jax.ShapeDtypeStruct((SUBY * CAP // 2, 128), jnp.float32),
        ),
        in_specs=[pl.BlockSpec(memory_space=pltpu.SMEM)] * 2 + [pl.BlockSpec(memory_space=pltpu.VMEM)] * 2,
        out_specs=(pl.BlockSpec(memory_space=pltpu.VMEM),) * 2,
        scratch_shapes=[
            pltpu.VMEM((SUBX * PLACES, 128), jnp.float32),
            pltpu.VMEM((2 * entries + 8, 128), jnp.float32),
        ],
        compiler_params=pltpu.CompilerParams(vmem_limit_bytes=8 * 1024 * 1024),
        name="place",
    )(info, index, *pieces)


def finish_kernel(arrived, wells):
    across = arrived[...].T
    lanes = lane_places()
    for start in range(0, ZONES, 8):
        low, high = across[start : start + 8], across[ZONES + start : ZONES + start + 8]
        for half in range(2):
            places = (half * 16 + lanes // CAP) * (CAP // 2) + lanes % (CAP // 2)
            both = [
                jnp.take_along_axis(part, places, axis=1, mode="promise_in_bounds") for part in (low, high)
            ]
            wells[start : start + 8, half * 128 : (half + 1) * 128] = jnp.where(
                lanes % CAP < CAP // 2, both[0], both[1]
            )


def run_finish(arrived):
    return pl.pallas_call(
        finish_kernel,
        out_shape=jax.ShapeDtypeStruct((ZONES, SUBY * CAP), jnp.float32),
        in_specs=[pl.BlockSpec(memory_space=pltpu.VMEM)],
        out_specs=pl.BlockSpec(memory_space=pltpu.VMEM),
        compiler_params=pltpu.CompilerParams(vmem_limit_bytes=4 * 1024 * 1024),
        name="finish",
    )(arrived)


def swap(array, axis, pairs):
    return lax.ppermute(array, axis, pairs)


def partners(shift):
    return [(i, i ^ shift) for i in range(SUBX)]


def gather_inputs(conductivity, storage, head_term, zone_id, layer_count, others):
    own = run_pack(layer_count, conductivity, storage, head_term, zone_id)
    inner = [(i, i ^ 1) for i in range(SUBY)]
    outer = [(i, i + 1) for i in range(1, SUBY - 1, 2)]
    outer = outer + [(j, i) for i, j in outer]
    wide = jnp.concatenate([own, swap(own, "gy", inner), swap(own, "gy", outer)], axis=0)
    wide, others = lax.optimization_barrier((wide, others))
    mine = jnp.concatenate([wide] + [swap(wide, "gx", partners(shift)) for shift in (2, 4, 6)], axis=0)
    return mine, swap(mine, "gx", partners(1)), others


def line_index(well_cell, well_count):
    cells = well_cell.T
    slots = jnp.arange(CAP, dtype=jnp.int32)[:, None]
    layer = cells & (LAYERS - 1)
    entries = PLACES * LAYERS // 2
    turned = (layer & 1) != (slots >= CAP // 2).astype(jnp.int32)
    lines = (layer >> 1) * PLACES + (cells >> 4) + jnp.where(turned, entries, 0)
    return jnp.where(slots < well_count[None, :], lines, 2 * entries)


def shards(conductivity, storage, head_term, zone_id, layer_count, well_cell, well_count):
    row, col = lax.axis_index("gx"), lax.axis_index("gy")
    info = jnp.stack([row, col, SUBY - 1 - col]).astype(jnp.int32)
    index = line_index(well_cell[0, 0], well_count[0, 0])
    mine, other, (info, index) = gather_inputs(
        conductivity, storage, head_term, zone_id, layer_count, (info, index)
    )
    sends = run_main(info, mine, other)
    near = [sends[0]] + [swap(sends[k], "gx", partners(2 * k)) for k in (1, 2, 3)]
    near = jnp.concatenate(near[::-1], axis=0)
    tangent, picks = run_place(info, index, (near, swap(near, "gx", partners(1))))
    picks = picks.reshape(SUBY, CAP // 2, 128)
    arrived = lax.all_to_all(picks, "gy", split_axis=0, concat_axis=0, tiled=True)
    wells = run_finish(arrived.reshape(SUBY * CAP // 2, 128)).T
    return (tangent.reshape(ROWS, COLS, LAYERS * ZONES), wells)


def solution(mesh):
    placed = (
        P("gx", "gy", None),
        P("gx", "gy", None),
        P("gx", "gy", None),
        P("gx", "gy", None),
        P("gx", "gy"),
        P("gx", "gy", None, None),
        P("gx", "gy", None),
    )
    return jax.shard_map(
        shards,
        mesh=mesh,
        in_specs=placed,
        out_specs=(P("gx", "gy", None), P(("gx", "gy"), None)),
        check_vma=False,
    )
```
